32 devices in a mesh: layer: 2 (over y), dp: 16 (over z, x, core).
Axes of the slice: x: 2, y: 2, z: 4, core: 2. Of those that a mesh axis runs over, the one named last changes fastest.
Arguments:
- states: bfloat16 [6, 32, 32, 32, 128], P('layer', 'dp'), may hold values from -6 to 6
- weights: bfloat16 [6, 1152, 128], P('layer'), may hold values from -0.1875 to 0.1875
- bias: float32 [6, 128], P('layer'), may hold values from -3 to 3
- guesses: float32 [2, 32, 32, 32, 128], P('layer', 'dp'), may hold values from -6 to 6
- coarse_gain: float32 [2, 128], replicated, may hold values from 0.5 to 1
Outputs:
- section_starts: float32 [2, 32, 32, 32, 128], P('layer', 'dp')
- weight_grad: float32 [6, 1152, 128], P('layer', 'dp')
- bias_grad: float32 [6, 128], P('layer', 'dp')
The draws below stay inside these ranges and needn't reach their ends.
All inputs are finite; a program needn't handle non-finite values.
Results may differ from the reference program's by a relative error of at most 0.007.
Values sent between devices are 32-bit elements; how exact they have to be, the bound alone decides.
A program may use at most 64 MiB of HBM per device.

```python
import math
import jax
import jax.numpy as jnp
from jax import lax

CH = 128
HGT = 32
WID = 32
L_SEC = 3
SECTIONS = 2
LAYERS = 6
IMAGES = 32


def raised(array, key, source, target, blocks, factor):
    def block_of(dim):
        return (jnp.arange(array.shape[dim]) // (array.shape[dim] // blocks)).reshape((-1,) + (1,) * (array.ndim - 1 - dim))

    one_side = jax.random.permutation(key, blocks)[block_of(target)]
    second = (block_of(target) + blocks // 2) % blocks
    return jnp.where((block_of(source) == one_side) | (block_of(source) == second), factor * array, array)


def shard_levels(rng, dims, shards, low, top_value):
    def one(axis_at, parts):
        steps = jax.random.uniform(jax.random.fold_in(jax.random.fold_in(rng, 6), axis_at), (parts,), jnp.float32, low / len(shards), top_value / len(shards))
        return jnp.repeat(jnp.exp(steps), dims[axis_at] // parts).reshape((-1,) + (1,) * (len(dims) - axis_at - 1))

    gain = one(*shards[0])
    for cut in shards[1:]:
        gain = gain * one(*cut)
    return gain


def noise(key, dims, scale, most, pieces=(), kind=jnp.bfloat16):
    loudness = shard_levels(key, dims, pieces, -0.22, 0.18) if pieces else 1.0
    drawn = jax.random.normal(key, dims, jnp.float32) * scale * loudness
    return jnp.minimum(jnp.maximum(drawn, -most), most).astype(kind)


def noise_with(rng, extent, width, bound, shards, heavy, held_as=jnp.bfloat16):
    result = width * jax.random.normal(rng, extent, jnp.float32)
    if shards:
        result = result * shard_levels(rng, extent, shards, -0.22, 0.18)
    return jnp.clip(raised(result, jax.random.fold_in(rng, 3), *heavy), -bound, bound).astype(held_as)


def setup_inputs(seed: int = 0) -> dict:
    splits = jax.random.split(jax.random.key(seed), 6)
    return {
        "states": noise_with(splits[0], (LAYERS, IMAGES, HGT, WID, CH), 1.0, 6.0, ((0, 2), (1, 16)), (1, 4, 16, 2.0)),
        "weights": noise(splits[1], (LAYERS, 9 * CH, CH), (9 * CH) ** -0.5, 0.1875, ((0, 2),)),
        "bias": noise(splits[2], (LAYERS, CH), 0.5, 3.0, ((0, 2),), jnp.float32),
        "guesses": noise(splits[3], (SECTIONS, IMAGES, HGT, WID, CH), 1.0, 6.0, ((0, 2), (1, 16)), jnp.float32),
        "coarse_gain": jnp.clip(jnp.exp(jax.random.uniform(splits[4], (SECTIONS, CH), jnp.float32, math.log(0.5), math.log(1.0))), 0.5, 1.0),
    }


step_size = 0.5
layout_names = ("NHWC", "HWIO", "NHWC")


def as_kernel(matrix):
    channels = matrix.shape[1]
    return matrix.reshape(3, 3, channels, channels)


def convolve(field, kernel):
    return lax.conv_general_dilated(field, kernel, (1, 1), ((1, 1), (1, 1)), dimension_numbers=layout_names, preferred_element_type=jnp.float32)


def transpose_conv(scaled, matrix):
    kernel = jnp.swapaxes(as_kernel(matrix)[::-1, ::-1], 2, 3)
    return convolve(scaled, kernel)


def weight_term(field, scaled):
    height = field.shape[1]
    breadth = field.shape[2]
    padded = jnp.pad(field, ((0, 0), (1, 1), (1, 1), (0, 0)))
    blocks = []
    for row_tap in range(3):
        for col_tap in range(3):
            window = padded[:, row_tap:row_tap + height, col_tap:col_tap + breadth, :]
            blocks.append(lax.dot_general(window, scaled, (((0, 1, 2), (0, 1, 2)), ((), ())), preferred_element_type=jnp.float32))
    return jnp.concatenate(blocks, axis=0)


def slopes(field, matrix, offset):
    value = jnp.tanh(convolve(field, as_kernel(matrix)) + offset)
    return 1.0 - value * value


def reference(states, weights, bias, guesses, coarse_gain):
    scale = step_size / IMAGES
    derivs = [slopes(states[layer], weights[layer], bias[layer]) for layer in range(LAYERS)]
    firsts = []
    for section in range(SECTIONS):
        adjoint = guesses[section]
        for position in reversed(range(L_SEC)):
            layer = section * L_SEC + position
            scaled = (derivs[layer] * adjoint).astype(jnp.bfloat16)
            adjoint = adjoint + step_size * transpose_conv(scaled, weights[layer])
        firsts.append(adjoint)
    carried = jnp.zeros_like(guesses[0])
    corrections = [carried] * SECTIONS
    for section in range(SECTIONS - 2, -1, -1):
        carried = (firsts[section + 1] - guesses[section]) + coarse_gain[section] * carried
        corrections[section] = carried
    starts = []
    weight_rows = [None] * LAYERS
    bias_rows = [None] * LAYERS
    for section in range(SECTIONS):
        adjoint = guesses[section] + corrections[section]
        for position in reversed(range(L_SEC)):
            layer = section * L_SEC + position
            scaled = (derivs[layer] * adjoint).astype(jnp.bfloat16)
            adjoint = adjoint + step_size * transpose_conv(scaled, weights[layer])
            weight_rows[layer] = scale * weight_term(states[layer], scaled)
            bias_rows[layer] = scale * jnp.sum(scaled, axis=(0, 1, 2), dtype=jnp.float32)
        starts.append(adjoint)
    return jnp.stack(starts), jnp.stack(weight_rows), jnp.stack(bias_rows)
```

```python
import functools

import jax
import jax.numpy as jnp
from jax import lax
from jax.experimental import pallas as pl
from jax.experimental.pallas import tpu as pltpu
from jax.sharding import PartitionSpec as P

MESH = pl.DeviceIdType.MESH
step_size = 0.5


def round_up(value, multiple):
    return -(-value // multiple) * multiple


def kernel(
    sections, peers, scale,
    states, weights, bias, guesses, gain,
    starts, weight_grad, bias_grad,
    x_in, w_in, g_in, wf, wt, x3, xt, slope, s3, adj, corr, msg, got, wacc, bacc,
    g, r1, h, r2, k, r3,
    w_sem, x_sem, g_sem, o_sem, m_send, m_recv,
    send1, recv1, send2, recv2, send3, recv3,
):
    depth, images, pairs, _, width, ch = states.shape
    depths = peers // 4
    block = weight_grad.shape[1]
    padded = round_up(block, 8)
    section = lax.axis_index("layer")
    me = lax.axis_index("dp")
    core = lax.rem(me, 2)
    col = lax.rem(lax.div(me, 2), 2)
    row = lax.div(me, 4)
    is_last = section == sections - 1
    not_last = section < sections - 1
    sends_on = section > 0

    def peer(row_at, col_at, core_at):
        return {"dp": (row_at * 2 + col_at) * 2 + core_at}

    around = [peer(row, col, 1 - core), peer(row, 1 - col, core)]
    around += [peer(lax.rem(row + hop, depths), col, core) for hop in range(1, depths)]

    barrier = pltpu.get_barrier_semaphore()
    for target in around:
        pl.semaphore_signal(barrier, inc=1, device_id=target, device_id_type=MESH)

    @pl.when(sends_on)
    def _():
        pl.semaphore_signal(barrier, inc=1, device_id={"layer": section - 1}, device_id_type=MESH)

    @pl.when(not_last)
    def _():
        pl.semaphore_signal(barrier, inc=1, device_id={"layer": section + 1}, device_id_type=MESH)

    def load_w(l):
        return pltpu.make_async_copy(weights.at[l], w_in.at[l], w_sem.at[l])

    def load_x(l, i):
        return pltpu.make_async_copy(states.at[l, i], x_in.at[l, i], x_sem.at[l, i])

    def load_g(i):
        return pltpu.make_async_copy(guesses.at[0, i], g_in.at[i], g_sem.at[i])

    for l in reversed(range(depth)):
        load_w(l).start()
        load_x(l, 0).start()
        if l == depth - 1:
            load_g(0).start()
    for i in range(1, images):
        for l in reversed(range(depth)):
            load_x(l, i).start()
        load_g(i).start()

    edge = jnp.zeros((width, 3 * ch), jnp.bfloat16)
    for l in range(depth):
        for i in range(images):
            for field in (x3, s3):
                field[l, i, 0, 0] = edge
                field[l, i, pairs, 1] = edge

    @pl.when(is_last)
    def _():
        corr[...] = jnp.zeros_like(corr)

    bacc[...] = jnp.zeros_like(bacc)

    @pl.loop(0, depth)
    def _(t):
        l = depth - 1 - t
        load_w(l).wait()
        wf[l, 0 : 9 * ch, 0:ch] = w_in[l]
        wf[l, 9 * ch : 12 * ch, 0:ch] = jnp.zeros((3 * ch, ch), jnp.bfloat16)
        wf[l, 0 : 3 * ch, ch : 2 * ch] = jnp.zeros((3 * ch, ch), jnp.bfloat16)
        wf[l, 3 * ch : 12 * ch, ch : 2 * ch] = w_in[l]
        for j in range(2):
            for r in range(4):
                for dx in range(3):
                    at = (r * 3 + dx) * ch
                    tap = (2 - (r - j)) * 3 + (2 - dx)
                    if 0 <= r - j <= 2:
                        part = w_in[l, tap * ch : (tap + 1) * ch, :]
                    else:
                        part = jnp.zeros((ch, ch), jnp.bfloat16)
                    wt[l, j * ch : (j + 1) * ch, at : at + ch] = part

    column = lax.broadcasted_iota(jnp.int32, (pairs, width, ch), 1)

    def spread(field, l, i, j, value):
        left = jnp.where(column == 0, 0.0, pltpu.roll(value, 1, 1))
        right = jnp.where(column == width - 1, 0.0, pltpu.roll(value, width - 1, 1))
        at = pl.ds(j, pairs)
        field[l, i, at, 1 - j, :, 0:ch] = left.astype(jnp.bfloat16)
        field[l, i, at, 1 - j, :, ch : 2 * ch] = value.astype(jnp.bfloat16)
        field[l, i, at, 1 - j, :, 2 * ch : 3 * ch] = right.astype(jnp.bfloat16)

    def windows(field, l, i):
        parts = [field[l, i, pl.ds(r // 2, pairs), r % 2] for r in range(4)]
        return jnp.concatenate(parts, axis=-1).reshape(pairs * width, 12 * ch)

    def slope_step(l, i):
        for j in range(2):
            spread(x3, l, i, j, x_in[l, i, :, j].astype(jnp.float32))
        out = lax.dot_general(
            windows(x3, l, i), wf[l], (((1,), (0,)), ((), ())), preferred_element_type=jnp.float32
        )
        offset = bias[pl.ds(l, 1), :]
        for j in range(2):
            value = jnp.tanh(out[:, j * ch : (j + 1) * ch] + offset)
            slope[l, i, :, j] = (1.0 - value * value).reshape(pairs, width, ch)

    def scale_step(l, i):
        for j in range(2):
            scaled = (slope[l, i, :, j] * adj[i, :, j]).astype(jnp.bfloat16).astype(jnp.float32)
            spread(s3, l, i, j, scaled)

    def adjoint_step(l, i):
        out = lax.dot_general(
            windows(s3, l, i), wt[l], (((1,), (1,)), ((), ())), preferred_element_type=jnp.float32
        )
        for j in range(2):
            part = out[:, j * ch : (j + 1) * ch].reshape(pairs, width, ch)
            adj[i, :, j] = adj[i, :, j] + step_size * part

    def turn_step(l, i):
        flat = [x3[l, i, pl.ds(j, pairs), 1 - j].reshape(pairs * width, 3 * ch) for j in range(2)]
        for j in range(2):
            xt[l, i, :, j * pairs * width : (j + 1) * pairs * width] = flat[j].T

    def grad_step(l, i, first):
        rows = []
        for j in range(2):
            parts = []
            for dy in range(3):
                r = j + 2 - dy
                parts.append(s3[l, i, pl.ds(r // 2, pairs), r % 2, :, ch : 2 * ch])
            rows.append(jnp.concatenate(parts, axis=-1).reshape(pairs * width, 3 * ch))
        right = jnp.concatenate(rows, axis=0)
        out = lax.dot_general(
            xt[l, i], right, (((1,), (0,)), ((), ())), preferred_element_type=jnp.float32
        )
        total = jnp.sum(right[:, ch : 2 * ch].astype(jnp.float32), axis=0, keepdims=True)
        bacc[pl.ds(l, 1), :] = bacc[pl.ds(l, 1), :] + total
        for dy in range(3):
            at = slice(dy * 3 * ch, (dy + 1) * 3 * ch)
            part = out[:, dy * ch : (dy + 1) * ch]
            wacc[l, at, :] = part if first else wacc[l, at, :] + part

    def message(i):
        return pltpu.make_async_remote_copy(
            src_ref=msg.at[i],
            dst_ref=got.at[i],
            send_sem=m_send.at[i],
            recv_sem=m_recv.at[i],
            device_id={"layer": section - 1},
            device_id_type=MESH,
        )

    def height(l):
        return padded if l else g.shape[4]

    def swap_cores(l):
        return pltpu.make_async_remote_copy(
            src_ref=g.at[l, 1 - core, :, :, 0 : height(l)],
            dst_ref=r1.at[l, :, :, 0 : height(l)],
            send_sem=send1.at[l],
            recv_sem=recv1.at[l],
            device_id=around[0],
            device_id_type=MESH,
        )

    def swap_cols(l):
        return pltpu.make_async_remote_copy(
            src_ref=h.at[l, 1 - col, :, 0 : height(l)],
            dst_ref=r2.at[l, :, 0 : height(l)],
            send_sem=send2.at[l],
            recv_sem=recv2.at[l],
            device_id=around[1],
            device_id_type=MESH,
        )

    def swap_rows(l, hop):
        return pltpu.make_async_remote_copy(
            src_ref=k.at[l, lax.rem(row + hop, depths), 0 : height(l)],
            dst_ref=r3.at[l, hop - 1, 0 : height(l)],
            send_sem=send3.at[l, hop - 1],
            recv_sem=recv3.at[l, hop - 1],
            device_id=around[1 + hop],
            device_id_type=MESH,
        )

    def reduce_1(l):
        for d in range(peers):
            at = (l, d % 2, (d // 2) % 2, d // 4)
            g[at + (slice(0, block),)] = wacc[l, d * block : (d + 1) * block, :]
            if l == 0:
                g[at + (slice(padded, None),)] = bacc[...]
        swap_cores(l).start()

    def reduce_2(l):
        n = height(l)
        swap_cores(l).wait_recv()
        h[l, 1 - col, :, 0:n] = g[l, core, 1 - col, :, 0:n] + r1[l, 1 - col, :, 0:n]
        swap_cols(l).start()
        h[l, col, :, 0:n] = g[l, core, col, :, 0:n] + r1[l, col, :, 0:n]

    def reduce_3(l):
        n = height(l)
        swap_cols(l).wait_recv()
        k[l, :, 0:n] = h[l, col, :, 0:n] + r2[l, :, 0:n]
        for hop in range(1, depths):
            swap_rows(l, hop).start()

    def reduce_4(l):
        n = height(l)
        total = k[l, row, 0:n]
        for hop in range(1, depths):
            swap_rows(l, hop).wait_recv()
            total = total + r3[l, hop - 1, 0:n]
        weight_grad[l] = scale * total[0:block]
        if l == 0:
            sums = total[padded : padded + depth]
            lane = lax.broadcasted_iota(jnp.int32, sums.shape, 1)
            share = bias_grad.shape[1]
            for at in range(share):
                mine = jnp.where(lane == me * share + at, sums, 0.0)
                bias_grad[:, at : at + 1] = scale * jnp.sum(mine, axis=1, keepdims=True)

    neighbours = sends_on.astype(jnp.int32) + not_last.astype(jnp.int32)
    pl.semaphore_wait(barrier, len(around) + neighbours)

    @pl.when(sends_on)
    def _():
        @pl.loop(0, images)
        def _(i):
            load_g(i).wait()
            adj[i] = g_in[i]

            @pl.loop(0, depth)
            def _(t):
                l = depth - 1 - t
                load_x(l, i).wait()
                slope_step(l, i)
                scale_step(l, i)
                adjoint_step(l, i)

            @pl.when(not_last)
            def _():
                message(i).wait_recv()
                corr[i] = got[i] - g_in[i]

            factor = gain[pl.ds(section - 1, 1), :].reshape(1, 1, 1, ch)
            msg[i] = adj[i] + factor * corr[i]
            message(i).start()

    @pl.when(jnp.logical_not(sends_on))
    def _():
        @pl.loop(0, images)
        def _(i):
            load_g(i).wait()

            @pl.loop(0, depth)
            def _(t):
                l = depth - 1 - t
                load_x(l, i).wait()
                slope_step(l, i)

    @pl.loop(0, images)
    def _(i):
        @pl.loop(0, depth)
        def _(l):
            turn_step(l, i)

    def begin(i):
        @pl.when(section == 0)
        def _():
            message(i).wait_recv()

        @pl.when(not_last)
        def _():
            adj[i] = got[i]

    def store(i):
        return pltpu.make_async_copy(adj.at[i], starts.at[0, i], o_sem.at[i])

    for i in range(images - 1):
        begin(i)

        @pl.loop(0, depth)
        def _(t):
            l = depth - 1 - t

            @pl.when(not_last)
            def _():
                scale_step(l, i)
                adjoint_step(l, i)

            grad_step(l, i, i == 0)

        store(i).start()

    i = images - 1
    begin(i)
    for l in reversed(range(depth)):
        @pl.when(not_last)
        def _():
            scale_step(l, i)

        grad_step(l, i, i == 0)
        reduce_1(l)

        @pl.when(not_last)
        def _():
            adjoint_step(l, i)

        reduce_2(l)
        if l < depth - 1:
            reduce_3(l + 1)
    store(i).start()
    reduce_3(0)
    for l in reversed(range(depth)):
        reduce_4(l)

    for i in range(images):
        store(i).wait()

        @pl.when(sends_on)
        def _():
            message(i).wait_send()

    for l in range(depth):
        swap_cores(l).wait_send()
        swap_cols(l).wait_send()
        for hop in range(1, depths):
            swap_rows(l, hop).wait_send()


def per_device(sections, peers, states, weights, bias, guesses, coarse_gain):
    depth, images, high, width, ch = states.shape
    pairs = high // 2
    rows = 9 * ch // peers
    depths = peers // 4
    tall = round_up(rows, 8) + round_up(depth, 8)
    scale = step_size / (images * peers)
    f32, bf16 = jnp.float32, jnp.bfloat16
    image = (images, pairs, 2, width, ch)
    taps = (depth, images, pairs + 1, 2, width, 3 * ch)
    dma = pltpu.SemaphoreType.DMA
    conv_flops = 2 * images * high * width * 9 * ch * ch
    vmem, anywhere = pl.BlockSpec(memory_space=pltpu.VMEM), pl.BlockSpec(memory_space=pl.ANY)
    starts, weight_grad, bias_grad = pl.pallas_call(
        functools.partial(kernel, sections, peers, scale),
        out_shape=(
            jax.ShapeDtypeStruct((1,) + image, f32),
            jax.ShapeDtypeStruct((depth, rows, ch), f32),
            jax.ShapeDtypeStruct((depth, ch // peers), f32),
        ),
        in_specs=[anywhere, anywhere, vmem, anywhere, vmem],
        out_specs=(anywhere, vmem, vmem),
        scratch_shapes=[
            pltpu.VMEM((depth,) + image, bf16),
            pltpu.VMEM((depth, 9 * ch, ch), bf16),
            pltpu.VMEM(image, f32),
            pltpu.VMEM((depth, 12 * ch, 2 * ch), bf16),
            pltpu.VMEM((depth, 2 * ch, 12 * ch), bf16),
            pltpu.VMEM(taps, bf16),
            pltpu.VMEM((depth, images, 3 * ch, high * width), bf16),
            pltpu.VMEM((depth,) + image, f32),
            pltpu.VMEM(taps, bf16),
            pltpu.VMEM(image, f32),
            pltpu.VMEM(image, f32),
            pltpu.VMEM(image, f32),
            pltpu.VMEM(image, f32),
            pltpu.VMEM((depth, 9 * ch, ch), f32),
            pltpu.VMEM((round_up(depth, 8), ch), f32),
            pltpu.VMEM((depth, 2, 2, depths, tall, ch), f32),
            pltpu.VMEM((depth, 2, depths, tall, ch), f32),
            pltpu.VMEM((depth, 2, depths, tall, ch), f32),
            pltpu.VMEM((depth, depths, tall, ch), f32),
            pltpu.VMEM((depth, depths, tall, ch), f32),
            pltpu.VMEM((depth, depths, tall, ch), f32),
            dma((depth,)), dma((depth, images)), dma((images,)), dma((images,)),
            dma((images,)), dma((images,)),
            dma((depth,)), dma((depth,)), dma((depth,)), dma((depth,)),
            dma((depth, depths)), dma((depth, depths)),
        ],
        compiler_params=pltpu.CompilerParams(
            collective_id=0, has_side_effects=True, vmem_limit_bytes=56 * 1024 * 1024
        ),
        cost_estimate=pl.CostEstimate(
            flops=9 * conv_flops, bytes_accessed=8 * states.size, transcendentals=states.size
        ),
    )(
        states.reshape((depth,) + image),
        weights,
        bias,
        guesses.reshape((1,) + image),
        coarse_gain,
    )
    return starts.reshape(guesses.shape), weight_grad, bias_grad


def solution(mesh):
    return jax.shard_map(
        functools.partial(per_device, mesh.shape["layer"], mesh.shape["dp"]),
        mesh=mesh,
        in_specs=(
            P("layer", "dp", None, None, None),
            P("layer", None, None),
            P("layer", None),
            P("layer", "dp", None, None, None),
            P(),
        ),
        out_specs=(P("layer", "dp", None, None, None), P("layer", "dp", None), P("layer", "dp")),
        check_vma=False,
    )
```

```python
import functools

import jax
import jax.numpy as jnp
from jax import lax
from jax.experimental import pallas as pl
from jax.experimental.pallas import tpu as pltpu
from jax.sharding import PartitionSpec as P

MESH = pl.DeviceIdType.MESH
step_size = 0.5


def round_up(value, multiple):
    return -(-value // multiple) * multiple


def kernel(
    sections, peers, scale,
    states, weights, bias, guesses, gain,
    starts, weight_grad, bias_grad,
    x_in, w_in, g_in, wf, wt, x3, xt, slope, s3, adj, corr, msg, got, wacc, bacc,
    g, r1, h, r2, k, r3,
    w_sem, x_sem, g_sem, o_sem, m_send, m_recv,
    send1, recv1, send2, recv2, send3, recv3,
):
    depth, images, pairs, _, width, ch = states.shape
    depths = peers // 4
    block = weight_grad.shape[1]
    padded = round_up(block, 8)
    section = lax.axis_index("layer")
    me = lax.axis_index("dp")
    core = lax.rem(me, 2)
    col = lax.rem(lax.div(me, 2), 2)
    row = lax.div(me, 4)
    is_last = section == sections - 1
    not_last = section < sections - 1
    sends_on = section > 0

    def peer(row_at, col_at, core_at):
        return {"dp": (row_at * 2 + col_at) * 2 + core_at}

    around = [peer(row, col, 1 - core), peer(row, 1 - col, core)]
    around += [peer(lax.rem(row + hop, depths), col, core) for hop in range(1, depths)]

    barrier = pltpu.get_barrier_semaphore()
    for target in around:
        pl.semaphore_signal(barrier, inc=1, device_id=target, device_id_type=MESH)

    @pl.when(sends_on)
    def _():
        pl.semaphore_signal(barrier, inc=1, device_id={"layer": section - 1}, device_id_type=MESH)

    @pl.when(not_last)
    def _():
        pl.semaphore_signal(barrier, inc=1, device_id={"layer": section + 1}, device_id_type=MESH)

    def load_w(l):
        return pltpu.make_async_copy(weights.at[l], w_in.at[l], w_sem.at[l])

    def load_x(l, i):
        return pltpu.make_async_copy(states.at[l, i], x_in.at[l, i], x_sem.at[l, i])

    def load_g(i):
        return pltpu.make_async_copy(guesses.at[0, i], g_in.at[i], g_sem.at[i])

    for l in reversed(range(depth)):
        load_w(l).start()
        load_x(l, 0).start()
        if l == depth - 1:
            load_g(0).start()
    for i in range(1, images):
        for l in reversed(range(depth)):
            load_x(l, i).start()
        load_g(i).start()

    edge = jnp.zeros((width, 3 * ch), jnp.bfloat16)
    for l in range(depth):
        for i in range(images):
            for field in (x3, s3):
                field[l, i, 0, 0] = edge
                field[l, i, pairs, 1] = edge

    @pl.when(is_last)
    def _():
        corr[...] = jnp.zeros_like(corr)

    bacc[...] = jnp.zeros_like(bacc)

    @pl.loop(0, depth)
    def _(t):
        l = depth - 1 - t
        load_w(l).wait()
        wf[l, 0 : 9 * ch, 0:ch] = w_in[l]
        wf[l, 9 * ch : 12 * ch, 0:ch] = jnp.zeros((3 * ch, ch), jnp.bfloat16)
        wf[l, 0 : 3 * ch, ch : 2 * ch] = jnp.zeros((3 * ch, ch), jnp.bfloat16)
        wf[l, 3 * ch : 12 * ch, ch : 2 * ch] = w_in[l]
        for tap in range(9):
            turned = w_in[l, tap * ch : (tap + 1) * ch, :].T
            dy, dx = 2 - tap // 3, 2 - tap % 3
            for j in range(2):
                at = ((dy + j) * 3 + dx) * ch
                wt[l, at : at + ch, j * ch : (j + 1) * ch] = turned
        wt[l, 9 * ch : 12 * ch, 0:ch] = jnp.zeros((3 * ch, ch), jnp.bfloat16)
        wt[l, 0 : 3 * ch, ch : 2 * ch] = jnp.zeros((3 * ch, ch), jnp.bfloat16)

    column = lax.broadcasted_iota(jnp.int32, (1, width, ch), 1)
    leftmost, rightmost = column == 0, column == width - 1
    chunk = 4
    chunks = [slice(q, q + chunk) for q in range(0, pairs, chunk)]

    def spread(field, l, i, j, q, value):
        left = jnp.where(leftmost, 0.0, pltpu.roll(value, 1, 1))
        right = jnp.where(rightmost, 0.0, pltpu.roll(value, width - 1, 1))
        at = slice(q.start + j, q.stop + j)
        field[l, i, at, 1 - j, :, 0:ch] = left.astype(jnp.bfloat16)
        field[l, i, at, 1 - j, :, ch : 2 * ch] = value.astype(jnp.bfloat16)
        field[l, i, at, 1 - j, :, 2 * ch : 3 * ch] = right.astype(jnp.bfloat16)

    def windows(field, l, i):
        parts = [field[l, i, pl.ds(r // 2, pairs), r % 2] for r in range(4)]
        return jnp.concatenate(parts, axis=-1).reshape(pairs * width, 12 * ch)

    def slope_step(l, i):
        for q in chunks:
            for j in range(2):
                spread(x3, l, i, j, q, x_in[l, i, q, j].astype(jnp.float32))
        out = lax.dot_general(
            windows(x3, l, i), wf[l], (((1,), (0,)), ((), ())), preferred_element_type=jnp.float32
        )
        offset = bias[pl.ds(l, 1), :]
        for q in chunks:
            for j in range(2):
                part = out[q.start * width : q.stop * width, j * ch : (j + 1) * ch]
                value = jnp.tanh(part + offset)
                slope[l, i, q, j] = (1.0 - value * value).reshape(chunk, width, ch)

    def scale_step(l, i):
        for q in chunks:
            for j in range(2):
                spread(s3, l, i, j, q, slope[l, i, q, j] * adj[i, q, j])

    def adjoint_step(l, i):
        out = lax.dot_general(
            windows(s3, l, i), wt[l], (((1,), (0,)), ((), ())), preferred_element_type=jnp.float32
        )
        for q in chunks:
            for j in range(2):
                part = out[q.start * width : q.stop * width, j * ch : (j + 1) * ch]
                adj[i, q, j] = adj[i, q, j] + step_size * part.reshape(chunk, width, ch)

    def turn_step(l, i):
        flat = [x3[l, i, pl.ds(j, pairs), 1 - j].reshape(pairs * width, 3 * ch) for j in range(2)]
        for j in range(2):
            xt[l, i, :, j * pairs * width : (j + 1) * pairs * width] = flat[j].T

    def grad_step(l, i, first):
        rows = []
        for j in range(2):
            parts = []
            for dy in range(3):
                r = j + 2 - dy
                parts.append(s3[l, i, pl.ds(r // 2, pairs), r % 2, :, ch : 2 * ch])
            rows.append(jnp.concatenate(parts, axis=-1).reshape(pairs * width, 3 * ch))
        right = jnp.concatenate(rows, axis=0)
        out = lax.dot_general(
            xt[l, i], right, (((1,), (0,)), ((), ())), preferred_element_type=jnp.float32
        )
        total = jnp.sum(right[:, ch : 2 * ch].astype(jnp.float32), axis=0, keepdims=True)
        bacc[pl.ds(l, 1), :] = bacc[pl.ds(l, 1), :] + total
        for dy in range(3):
            at = slice(dy * 3 * ch, (dy + 1) * 3 * ch)
            part = out[:, dy * ch : (dy + 1) * ch]
            wacc[l, at, :] = part if first else wacc[l, at, :] + part

    def message(i):
        return pltpu.make_async_remote_copy(
            src_ref=msg.at[i],
            dst_ref=got.at[i],
            send_sem=m_send.at[i],
            recv_sem=m_recv.at[i],
            device_id={"layer": section - 1},
            device_id_type=MESH,
        )

    def height(l):
        return padded if l else g.shape[4]

    def swap_cores(l):
        return pltpu.make_async_remote_copy(
            src_ref=g.at[l, 1 - core, :, :, 0 : height(l)],
            dst_ref=r1.at[l, :, :, 0 : height(l)],
            send_sem=send1.at[l],
            recv_sem=recv1.at[l],
            device_id=around[0],
            device_id_type=MESH,
        )

    def swap_cols(l):
        return pltpu.make_async_remote_copy(
            src_ref=h.at[l, 1 - col, :, 0 : height(l)],
            dst_ref=r2.at[l, :, 0 : height(l)],
            send_sem=send2.at[l],
            recv_sem=recv2.at[l],
            device_id=around[1],
            device_id_type=MESH,
        )

    def swap_rows(l, hop):
        return pltpu.make_async_remote_copy(
            src_ref=k.at[l, lax.rem(row + hop, depths), 0 : height(l)],
            dst_ref=r3.at[l, hop - 1, 0 : height(l)],
            send_sem=send3.at[l, hop - 1],
            recv_sem=recv3.at[l, hop - 1],
            device_id=around[1 + hop],
            device_id_type=MESH,
        )

    def reduce_1(l):
        for d in range(peers):
            at = (l, d % 2, (d // 2) % 2, d // 4)
            g[at + (slice(0, block),)] = wacc[l, d * block : (d + 1) * block, :]
            if l == 0:
                g[at + (slice(padded, None),)] = bacc[...]
        swap_cores(l).start()

    def reduce_2(l):
        n = height(l)
        swap_cores(l).wait_recv()
        h[l, 1 - col, :, 0:n] = g[l, core, 1 - col, :, 0:n] + r1[l, 1 - col, :, 0:n]
        swap_cols(l).start()
        h[l, col, :, 0:n] = g[l, core, col, :, 0:n] + r1[l, col, :, 0:n]

    def reduce_3(l):
        n = height(l)
        swap_cols(l).wait_recv()
        k[l, :, 0:n] = h[l, col, :, 0:n] + r2[l, :, 0:n]
        for hop in range(1, depths):
            swap_rows(l, hop).start()

    def reduce_4(l):
        n = height(l)
        total = k[l, row, 0:n]
        for hop in range(1, depths):
            swap_rows(l, hop).wait_recv()
            total = total + r3[l, hop - 1, 0:n]
        weight_grad[l] = scale * total[0:block]
        if l == 0:
            sums = total[padded : padded + depth]
            lane = lax.broadcasted_iota(jnp.int32, sums.shape, 1)
            share = bias_grad.shape[1]
            for at in range(share):
                mine = jnp.where(lane == me * share + at, sums, 0.0)
                bias_grad[:, at : at + 1] = scale * jnp.sum(mine, axis=1, keepdims=True)

    neighbours = sends_on.astype(jnp.int32) + not_last.astype(jnp.int32)
    pl.semaphore_wait(barrier, len(around) + neighbours)

    @pl.when(sends_on)
    def _():
        @pl.loop(0, images)
        def _(i):
            load_g(i).wait()
            adj[i] = g_in[i]

            @pl.loop(0, depth)
            def _(t):
                l = depth - 1 - t
                load_x(l, i).wait()
                slope_step(l, i)
                scale_step(l, i)
                adjoint_step(l, i)

            @pl.when(not_last)
            def _():
                message(i).wait_recv()
                corr[i] = got[i] - g_in[i]

            factor = gain[pl.ds(section - 1, 1), :].reshape(1, 1, 1, ch)
            msg[i] = adj[i] + factor * corr[i]
            message(i).start()

    @pl.when(jnp.logical_not(sends_on))
    def _():
        @pl.loop(0, images)
        def _(i):
            load_g(i).wait()

            @pl.loop(0, depth)
            def _(t):
                l = depth - 1 - t
                load_x(l, i).wait()
                slope_step(l, i)

    @pl.loop(0, images)
    def _(i):
        @pl.loop(0, depth)
        def _(l):
            turn_step(l, i)

    def begin(i):
        @pl.when(section == 0)
        def _():
            message(i).wait_recv()

        @pl.when(not_last)
        def _():
            adj[i] = got[i]

    def store(i):
        return pltpu.make_async_copy(adj.at[i], starts.at[0, i], o_sem.at[i])

    for i in range(images - 1):
        begin(i)

        @pl.loop(0, depth)
        def _(t):
            l = depth - 1 - t

            @pl.when(not_last)
            def _():
                scale_step(l, i)
                adjoint_step(l, i)

            grad_step(l, i, i == 0)

        store(i).start()

    i = images - 1
    begin(i)
    for l in reversed(range(depth)):
        @pl.when(not_last)
        def _():
            scale_step(l, i)

        grad_step(l, i, i == 0)
        reduce_1(l)

        @pl.when(not_last)
        def _():
            adjoint_step(l, i)

        reduce_2(l)
        if l < depth - 1:
            reduce_3(l + 1)
    store(i).start()
    reduce_3(0)
    for l in reversed(range(depth)):
        reduce_4(l)

    for i in range(images):
        store(i).wait()

        @pl.when(sends_on)
        def _():
            message(i).wait_send()

    for l in range(depth):
        swap_cores(l).wait_send()
        swap_cols(l).wait_send()
        for hop in range(1, depths):
            swap_rows(l, hop).wait_send()


def hand_over(parts, starts, weight_grad, bias_grad, starts_out, weight_out, bias_out, sem):
    per_image = parts // starts.shape[1]
    some = starts.shape[2] // per_image
    copies = []
    for part in range(parts):
        at = (0, part // per_image, pl.ds(part % per_image * some, some))
        copies.append(pltpu.make_async_copy(starts.at[at], starts_out.at[at], sem.at[part]))
    copies.append(pltpu.make_async_copy(weight_grad, weight_out, sem.at[parts]))
    copies.append(pltpu.make_async_copy(bias_grad, bias_out, sem.at[parts + 1]))
    for copy in copies:
        copy.start()
    for copy in copies:
        copy.wait()


def per_device(sections, peers, states, weights, bias, guesses, coarse_gain):
    depth, images, high, width, ch = states.shape
    pairs = high // 2
    rows = 9 * ch // peers
    depths = peers // 4
    tall = round_up(rows, 8) + round_up(depth, 8)
    scale = step_size / (images * peers)
    f32, bf16 = jnp.float32, jnp.bfloat16
    image = (images, pairs, 2, width, ch)
    taps = (depth, images, pairs + 1, 2, width, 3 * ch)
    dma = pltpu.SemaphoreType.DMA
    conv_flops = 2 * images * high * width * 9 * ch * ch
    vmem, anywhere = pl.BlockSpec(memory_space=pltpu.VMEM), pl.BlockSpec(memory_space=pl.ANY)
    starts, weight_grad, bias_grad = pl.pallas_call(
        functools.partial(kernel, sections, peers, scale),
        out_shape=(
            jax.ShapeDtypeStruct((1,) + image, f32),
            jax.ShapeDtypeStruct((depth, rows, ch), f32),
            jax.ShapeDtypeStruct((depth, ch // peers), f32),
        ),
        in_specs=[anywhere, anywhere, vmem, anywhere, vmem],
        out_specs=(anywhere, vmem, vmem),
        scratch_shapes=[
            pltpu.VMEM((depth,) + image, bf16),
            pltpu.VMEM((depth, 9 * ch, ch), bf16),
            pltpu.VMEM(image, f32),
            pltpu.VMEM((depth, 12 * ch, 2 * ch), bf16),
            pltpu.VMEM((depth, 12 * ch, 2 * ch), bf16),
            pltpu.VMEM(taps, bf16),
            pltpu.VMEM((depth, images, 3 * ch, high * width), bf16),
            pltpu.VMEM((depth,) + image, f32),
            pltpu.VMEM(taps, bf16),
            pltpu.VMEM(image, f32),
            pltpu.VMEM(image, f32),
            pltpu.VMEM(image, f32),
            pltpu.VMEM(image, f32),
            pltpu.VMEM((depth, 9 * ch, ch), f32),
            pltpu.VMEM((round_up(depth, 8), ch), f32),
            pltpu.VMEM((depth, 2, 2, depths, tall, ch), f32),
            pltpu.VMEM((depth, 2, depths, tall, ch), f32),
            pltpu.VMEM((depth, 2, depths, tall, ch), f32),
            pltpu.VMEM((depth, depths, tall, ch), f32),
            pltpu.VMEM((depth, depths, tall, ch), f32),
            pltpu.VMEM((depth, depths, tall, ch), f32),
            dma((depth,)), dma((depth, images)), dma((images,)), dma((images,)),
            dma((images,)), dma((images,)),
            dma((depth,)), dma((depth,)), dma((depth,)), dma((depth,)),
            dma((depth, depths)), dma((depth, depths)),
        ],
        compiler_params=pltpu.CompilerParams(
            collective_id=0, has_side_effects=True, vmem_limit_bytes=56 * 1024 * 1024
        ),
        cost_estimate=pl.CostEstimate(
            flops=9 * conv_flops, bytes_accessed=8 * states.size, transcendentals=states.size
        ),
    )(
        states.reshape((depth,) + image),
        weights,
        bias,
        guesses.reshape((1,) + image),
        coarse_gain,
    )
    parts = images * 4
    starts, weight_grad, bias_grad = pl.pallas_call(
        functools.partial(hand_over, parts),
        out_shape=(
            jax.ShapeDtypeStruct(starts.shape, f32),
            jax.ShapeDtypeStruct(weight_grad.shape, f32),
            jax.ShapeDtypeStruct(bias_grad.shape, f32),
        ),
        in_specs=[anywhere] * 3,
        out_specs=(anywhere,) * 3,
        scratch_shapes=[dma((parts + 2,))],
        compiler_params=pltpu.CompilerParams(vmem_limit_bytes=56 * 1024 * 1024),
    )(starts, weight_grad, bias_grad)
    return starts.reshape(guesses.shape), weight_grad, bias_grad


def solution(mesh):
    return jax.shard_map(
        functools.partial(per_device, mesh.shape["layer"], mesh.shape["dp"]),
        mesh=mesh,
        in_specs=(
            P("layer", "dp", None, None, None),
            P("layer", None, None),
            P("layer", None),
            P("layer", "dp", None, None, None),
            P(),
        ),
        out_specs=(P("layer", "dp", None, None, None), P("layer", "dp", None), P("layer", "dp")),
        check_vma=False,
    )
```

```python
import functools

import jax
import jax.numpy as jnp
from jax import lax
from jax.experimental import pallas as pl
from jax.experimental.pallas import tpu as pltpu
from jax.sharding import PartitionSpec as P

MESH = pl.DeviceIdType.MESH
step_size = 0.5


def round_up(value, multiple):
    return -(-value // multiple) * multiple


def kernel(
    sections, peers, scale,
    states, weights, bias, guesses, gain,
    starts, weight_grad, bias_grad,
    x_in, w_in, g_in, wf, wt, x3, xt, slope, s3, adj, corr, msg, got, wacc, bacc,
    g, r1, h, r2, k, r3,
    w_sem, x_sem, g_sem, o_sem, m_send, m_recv,
    send1, recv1, send2, recv2, send3, recv3,
):
    depth, images, pairs, _, width, ch = states.shape
    depths = peers // 4
    block = weight_grad.shape[1]
    padded = round_up(block, 8)
    section = lax.axis_index("layer")
    me = lax.axis_index("dp")
    core = lax.rem(me, 2)
    col = lax.rem(lax.div(me, 2), 2)
    row = lax.div(me, 4)
    is_last = section == sections - 1
    not_last = section < sections - 1
    sends_on = section > 0

    def peer(row_at, col_at, core_at):
        return {"dp": (row_at * 2 + col_at) * 2 + core_at}

    around = [peer(row, col, 1 - core), peer(row, 1 - col, core)]
    around += [peer(lax.rem(row + hop, depths), col, core) for hop in range(1, depths)]

    barrier = pltpu.get_barrier_semaphore()
    for target in around:
        pl.semaphore_signal(barrier, inc=1, device_id=target, device_id_type=MESH)

    @pl.when(sends_on)
    def _():
        pl.semaphore_signal(barrier, inc=1, device_id={"layer": section - 1}, device_id_type=MESH)

    @pl.when(not_last)
    def _():
        pl.semaphore_signal(barrier, inc=1, device_id={"layer": section + 1}, device_id_type=MESH)

    def load_w(l):
        return pltpu.make_async_copy(weights.at[l], w_in.at[l], w_sem.at[l])

    def load_x(l, i):
        return pltpu.make_async_copy(states.at[l, i], x_in.at[l, i], x_sem.at[l, i])

    def load_g(i):
        return pltpu.make_async_copy(guesses.at[0, i], g_in.at[i], g_sem.at[i])

    for l in reversed(range(depth)):
        load_w(l).start()
        load_x(l, 0).start()
        if l == depth - 1:
            load_g(0).start()
    for i in range(1, images):
        for l in reversed(range(depth)):
            load_x(l, i).start()
        load_g(i).start()

    edge = jnp.zeros((width, 3 * ch), jnp.bfloat16)
    for l in range(depth):
        for i in range(images):
            for field in (x3, s3):
                field[l, i, 0, 0] = edge
                field[l, i, pairs, 1] = edge

    @pl.when(is_last)
    def _():
        corr[...] = jnp.zeros_like(corr)

    bacc[...] = jnp.zeros_like(bacc)

    @pl.loop(0, depth)
    def _(t):
        l = depth - 1 - t
        load_w(l).wait()
        wf[l, 0 : 9 * ch, 0:ch] = w_in[l]
        wf[l, 9 * ch : 12 * ch, 0:ch] = jnp.zeros((3 * ch, ch), jnp.bfloat16)
        wf[l, 0 : 3 * ch, ch : 2 * ch] = jnp.zeros((3 * ch, ch), jnp.bfloat16)
        wf[l, 3 * ch : 12 * ch, ch : 2 * ch] = w_in[l]
        for tap in range(9):
            turned = w_in[l, tap * ch : (tap + 1) * ch, :].T
            dy, dx = 2 - tap // 3, 2 - tap % 3
            for j in range(2):
                at = ((dy + j) * 3 + dx) * ch
                wt[l, at : at + ch, j * ch : (j + 1) * ch] = turned
        wt[l, 9 * ch : 12 * ch, 0:ch] = jnp.zeros((3 * ch, ch), jnp.bfloat16)
        wt[l, 0 : 3 * ch, ch : 2 * ch] = jnp.zeros((3 * ch, ch), jnp.bfloat16)

    column = lax.broadcasted_iota(jnp.int32, (1, width, ch), 1)
    leftmost, rightmost = column == 0, column == width - 1
    chunk = 4
    chunks = [slice(q, q + chunk) for q in range(0, pairs, chunk)]

    def spread(field, l, i, j, q, value):
        left = jnp.where(leftmost, 0.0, pltpu.roll(value, 1, 1))
        right = jnp.where(rightmost, 0.0, pltpu.roll(value, width - 1, 1))
        at = slice(q.start + j, q.stop + j)
        field[l, i, at, 1 - j, :, 0:ch] = left.astype(jnp.bfloat16)
        field[l, i, at, 1 - j, :, ch : 2 * ch] = value.astype(jnp.bfloat16)
        field[l, i, at, 1 - j, :, 2 * ch : 3 * ch] = right.astype(jnp.bfloat16)

    def windows(field, l, i):
        parts = [field[l, i, pl.ds(r // 2, pairs), r % 2] for r in range(4)]
        return jnp.concatenate(parts, axis=-1).reshape(pairs * width, 12 * ch)

    def slope_step(l, i):
        for q in chunks:
            for j in range(2):
                spread(x3, l, i, j, q, x_in[l, i, q, j].astype(jnp.float32))
        out = lax.dot_general(
            windows(x3, l, i), wf[l], (((1,), (0,)), ((), ())), preferred_element_type=jnp.float32
        )
        offset = bias[pl.ds(l, 1), :]
        for q in chunks:
            for j in range(2):
                part = out[q.start * width : q.stop * width, j * ch : (j + 1) * ch]
                value = jnp.tanh(part + offset)
                slope[l, i, q, j] = (1.0 - value * value).reshape(chunk, width, ch)

    def scale_step(l, i):
        for q in chunks:
            for j in range(2):
                spread(s3, l, i, j, q, slope[l, i, q, j] * adj[i, q, j])

    def adjoint_step(l, i):
        out = lax.dot_general(
            windows(s3, l, i), wt[l], (((1,), (0,)), ((), ())), preferred_element_type=jnp.float32
        )
        for q in chunks:
            for j in range(2):
                part = out[q.start * width : q.stop * width, j * ch : (j + 1) * ch]
                adj[i, q, j] = adj[i, q, j] + step_size * part.reshape(chunk, width, ch)

    def turn_step(l, i):
        flat = [x3[l, i, pl.ds(j, pairs), 1 - j].reshape(pairs * width, 3 * ch) for j in range(2)]
        for j in range(2):
            xt[l, i, :, j * pairs * width : (j + 1) * pairs * width] = flat[j].T

    def grad_step(l, i, first):
        rows = []
        for j in range(2):
            parts = []
            for dy in range(3):
                r = j + 2 - dy
                parts.append(s3[l, i, pl.ds(r // 2, pairs), r % 2, :, ch : 2 * ch])
            rows.append(jnp.concatenate(parts, axis=-1).reshape(pairs * width, 3 * ch))
        right = jnp.concatenate(rows, axis=0)
        out = lax.dot_general(
            xt[l, i], right, (((1,), (0,)), ((), ())), preferred_element_type=jnp.float32
        )
        total = jnp.sum(right[:, ch : 2 * ch].astype(jnp.float32), axis=0, keepdims=True)
        bacc[pl.ds(l, 1), :] = bacc[pl.ds(l, 1), :] + total
        for dy in range(3):
            at = slice(dy * 3 * ch, (dy + 1) * 3 * ch)
            part = out[:, dy * ch : (dy + 1) * ch]
            wacc[l, at, :] = part if first else wacc[l, at, :] + part

    pieces = 4
    piece = pairs // pieces

    class message:
        def __init__(self, i):
            self.copies = [
                pltpu.make_async_remote_copy(
                    src_ref=msg.at[i, pl.ds(at * piece, piece)],
                    dst_ref=got.at[i, pl.ds(at * piece, piece)],
                    send_sem=m_send.at[i, at],
                    recv_sem=m_recv.at[i, at],
                    device_id={"layer": section - 1},
                    device_id_type=MESH,
                )
                for at in range(pieces)
            ]

        def start(self):
            for copy in self.copies:
                copy.start()

        def wait_recv(self):
            for copy in self.copies:
                copy.wait_recv()

        def wait_send(self):
            for copy in self.copies:
                copy.wait_send()

    def height(l):
        return padded if l else g.shape[4]

    def swap_cores(l):
        return pltpu.make_async_remote_copy(
            src_ref=g.at[l, 1 - core, :, :, 0 : height(l)],
            dst_ref=r1.at[l, :, :, 0 : height(l)],
            send_sem=send1.at[l],
            recv_sem=recv1.at[l],
            device_id=around[0],
            device_id_type=MESH,
        )

    def swap_cols(l):
        return pltpu.make_async_remote_copy(
            src_ref=h.at[l, 1 - col, :, 0 : height(l)],
            dst_ref=r2.at[l, :, 0 : height(l)],
            send_sem=send2.at[l],
            recv_sem=recv2.at[l],
            device_id=around[1],
            device_id_type=MESH,
        )

    def swap_rows(l, hop):
        return pltpu.make_async_remote_copy(
            src_ref=k.at[l, lax.rem(row + hop, depths), 0 : height(l)],
            dst_ref=r3.at[l, hop - 1, 0 : height(l)],
            send_sem=send3.at[l, hop - 1],
            recv_sem=recv3.at[l, hop - 1],
            device_id=around[1 + hop],
            device_id_type=MESH,
        )

    def reduce_1(l):
        for d in range(peers):
            at = (l, d % 2, (d // 2) % 2, d // 4)
            g[at + (slice(0, block),)] = wacc[l, d * block : (d + 1) * block, :]
            if l == 0:
                g[at + (slice(padded, None),)] = bacc[...]
        swap_cores(l).start()

    def reduce_2(l):
        n = height(l)
        swap_cores(l).wait_recv()
        h[l, 1 - col, :, 0:n] = g[l, core, 1 - col, :, 0:n] + r1[l, 1 - col, :, 0:n]
        swap_cols(l).start()
        h[l, col, :, 0:n] = g[l, core, col, :, 0:n] + r1[l, col, :, 0:n]

    def reduce_3(l):
        n = height(l)
        swap_cols(l).wait_recv()
        k[l, :, 0:n] = h[l, col, :, 0:n] + r2[l, :, 0:n]
        for hop in range(1, depths):
            swap_rows(l, hop).start()

    def reduce_4(l):
        n = height(l)
        total = k[l, row, 0:n]
        for hop in range(1, depths):
            swap_rows(l, hop).wait_recv()
            total = total + r3[l, hop - 1, 0:n]
        weight_grad[l] = scale * total[0:block]
        if l == 0:
            sums = total[padded : padded + depth]
            lane = lax.broadcasted_iota(jnp.int32, sums.shape, 1)
            share = bias_grad.shape[1]
            for at in range(share):
                mine = jnp.where(lane == me * share + at, sums, 0.0)
                bias_grad[:, at : at + 1] = scale * jnp.sum(mine, axis=1, keepdims=True)

    neighbours = sends_on.astype(jnp.int32) + not_last.astype(jnp.int32)
    pl.semaphore_wait(barrier, len(around) + neighbours)

    @pl.when(sends_on)
    def _():
        @pl.loop(0, images)
        def _(i):
            load_g(i).wait()
            adj[i] = g_in[i]

            @pl.loop(0, depth)
            def _(t):
                l = depth - 1 - t
                load_x(l, i).wait()
                slope_step(l, i)
                scale_step(l, i)
                adjoint_step(l, i)

            @pl.when(not_last)
            def _():
                message(i).wait_recv()
                corr[i] = got[i] - g_in[i]

            factor = gain[pl.ds(section - 1, 1), :].reshape(1, 1, 1, ch)
            msg[i] = adj[i] + factor * corr[i]
            message(i).start()

    @pl.when(jnp.logical_not(sends_on))
    def _():
        @pl.loop(0, images)
        def _(i):
            load_g(i).wait()

            @pl.loop(0, depth)
            def _(t):
                l = depth - 1 - t
                load_x(l, i).wait()
                slope_step(l, i)

    @pl.loop(0, images)
    def _(i):
        @pl.loop(0, depth)
        def _(l):
            turn_step(l, i)

    def begin(i):
        @pl.when(section == 0)
        def _():
            message(i).wait_recv()

        @pl.when(not_last)
        def _():
            adj[i] = got[i]

    def store(i):
        return pltpu.make_async_copy(adj.at[i], starts.at[0, i], o_sem.at[i])

    for i in range(images - 1):
        begin(i)

        @pl.loop(0, depth)
        def _(t):
            l = depth - 1 - t

            @pl.when(not_last)
            def _():
                scale_step(l, i)
                adjoint_step(l, i)

            grad_step(l, i, i == 0)

        store(i).start()

    i = images - 1
    begin(i)
    for l in reversed(range(depth)):
        @pl.when(not_last)
        def _():
            scale_step(l, i)

        grad_step(l, i, i == 0)
        reduce_1(l)

        @pl.when(not_last)
        def _():
            adjoint_step(l, i)

        reduce_2(l)
        if l < depth - 1:
            reduce_3(l + 1)
    store(i).start()
    reduce_3(0)
    for l in reversed(range(depth)):
        reduce_4(l)

    for i in range(images):
        store(i).wait()

        @pl.when(sends_on)
        def _():
            message(i).wait_send()

    for l in range(depth):
        swap_cores(l).wait_send()
        swap_cols(l).wait_send()
        for hop in range(1, depths):
            swap_rows(l, hop).wait_send()


def hand_over(starts, weight_grad, bias_grad, starts_out, weight_out, bias_out, held, in_sem, out_sem):
    images, pairs = starts.shape[1:3]
    parts = 4 if pairs % 4 == 0 else 1
    some = pairs // parts
    loads, stores = [], []
    for i in range(images):
        for part in range(parts):
            at, n = (0, i, pl.ds(part * some, some)), i * parts + part
            loads.append(pltpu.make_async_copy(starts.at[at], held.at[at], in_sem.at[n]))
            stores.append(pltpu.make_async_copy(held.at[at], starts_out.at[at], out_sem.at[n]))
    for load in loads:
        load.start()
    weight_out[...] = weight_grad[...]
    bias_out[...] = bias_grad[...]
    for load, store in zip(loads, stores):
        load.wait()
        store.start()
    for store in stores:
        store.wait()


def per_device(sections, peers, states, weights, bias, guesses, coarse_gain):
    depth, images, high, width, ch = states.shape
    pairs = high // 2
    rows = 9 * ch // peers
    depths = peers // 4
    tall = round_up(rows, 8) + round_up(depth, 8)
    scale = step_size / (images * peers)
    f32, bf16 = jnp.float32, jnp.bfloat16
    image = (images, pairs, 2, width, ch)
    taps = (depth, images, pairs + 1, 2, width, 3 * ch)
    dma = pltpu.SemaphoreType.DMA
    conv_flops = 2 * images * high * width * 9 * ch * ch
    vmem, anywhere = pl.BlockSpec(memory_space=pltpu.VMEM), pl.BlockSpec(memory_space=pl.ANY)
    starts, weight_grad, bias_grad = pl.pallas_call(
        functools.partial(kernel, sections, peers, scale),
        out_shape=(
            jax.ShapeDtypeStruct((1,) + image, f32),
            jax.ShapeDtypeStruct((depth, rows, ch), f32),
            jax.ShapeDtypeStruct((depth, ch // peers), f32),
        ),
        in_specs=[anywhere, anywhere, vmem, anywhere, vmem],
        out_specs=(anywhere, vmem, vmem),
        scratch_shapes=[
            pltpu.VMEM((depth,) + image, bf16),
            pltpu.VMEM((depth, 9 * ch, ch), bf16),
            pltpu.VMEM(image, f32),
            pltpu.VMEM((depth, 12 * ch, 2 * ch), bf16),
            pltpu.VMEM((depth, 12 * ch, 2 * ch), bf16),
            pltpu.VMEM(taps, bf16),
            pltpu.VMEM((depth, images, 3 * ch, high * width), bf16),
            pltpu.VMEM((depth,) + image, f32),
            pltpu.VMEM(taps, bf16),
            pltpu.VMEM(image, f32),
            pltpu.VMEM(image, f32),
            pltpu.VMEM(image, f32),
            pltpu.VMEM(image, f32),
            pltpu.VMEM((depth, 9 * ch, ch), f32),
            pltpu.VMEM((round_up(depth, 8), ch), f32),
            pltpu.VMEM((depth, 2, 2, depths, tall, ch), f32),
            pltpu.VMEM((depth, 2, depths, tall, ch), f32),
            pltpu.VMEM((depth, 2, depths, tall, ch), f32),
            pltpu.VMEM((depth, depths, tall, ch), f32),
            pltpu.VMEM((depth, depths, tall, ch), f32),
            pltpu.VMEM((depth, depths, tall, ch), f32),
            dma((depth,)), dma((depth, images)), dma((images,)), dma((images,)),
            dma((images, 4)), dma((images, 4)),
            dma((depth,)), dma((depth,)), dma((depth,)), dma((depth,)),
            dma((depth, depths)), dma((depth, depths)),
        ],
        compiler_params=pltpu.CompilerParams(
            collective_id=0, has_side_effects=True, vmem_limit_bytes=56 * 1024 * 1024
        ),
        cost_estimate=pl.CostEstimate(
            flops=9 * conv_flops, bytes_accessed=8 * states.size, transcendentals=states.size
        ),
    )(
        states.reshape((depth,) + image),
        weights,
        bias,
        guesses.reshape((1,) + image),
        coarse_gain,
    )
    starts, weight_grad, bias_grad = pl.pallas_call(
        hand_over,
        out_shape=(
            jax.ShapeDtypeStruct(starts.shape, f32),
            jax.ShapeDtypeStruct(weight_grad.shape, f32),
            jax.ShapeDtypeStruct(bias_grad.shape, f32),
        ),
        in_specs=[anywhere, vmem, vmem],
        out_specs=(anywhere, vmem, vmem),
        scratch_shapes=[pltpu.VMEM(starts.shape, f32), dma((images * 4,)), dma((images * 4,))],
        compiler_params=pltpu.CompilerParams(vmem_limit_bytes=60 * 1024 * 1024),
    )(starts, weight_grad, bias_grad)
    return starts.reshape(guesses.shape), weight_grad, bias_grad


def solution(mesh):
    return jax.shard_map(
        functools.partial(per_device, mesh.shape["layer"], mesh.shape["dp"]),
        mesh=mesh,
        in_specs=(
            P("layer", "dp", None, None, None),
            P("layer", None, None),
            P("layer", None),
            P("layer", "dp", None, None, None),
            P(),
        ),
        out_specs=(P("layer", "dp", None, None, None), P("layer", "dp", None), P("layer", "dp")),
        check_vma=False,
    )
```

```python
import functools

import jax
import jax.numpy as jnp
from jax import lax
from jax.experimental import pallas as pl
from jax.experimental.pallas import tpu as pltpu
from jax.sharding import PartitionSpec as P

MESH = pl.DeviceIdType.MESH
step_size = 0.5


def round_up(value, multiple):
    return -(-value // multiple) * multiple


def kernel(
    sections, peers, scale,
    states, weights, bias, guesses, gain,
    starts, weight_grad, bias_grad,
    x_in, w_in, g_in, wf, wt, x3, xt, slope, s3, adj, corr, msg, got, wacc, bacc,
    g, r1, h, r2, k, r3,
    w_sem, x_sem, g_sem, o_sem, m_send, m_recv,
    send1, recv1, send2, recv2, send3, recv3,
):
    depth, images, pairs, _, width, ch = states.shape
    depths = peers // 4
    block = weight_grad.shape[1]
    padded = round_up(block, 8)
    section = lax.axis_index("layer")
    me = lax.axis_index("dp")
    core = lax.rem(me, 2)
    col = lax.rem(lax.div(me, 2), 2)
    row = lax.div(me, 4)
    is_last = section == sections - 1
    not_last = section < sections - 1
    sends_on = section > 0

    def peer(row_at, col_at, core_at):
        return {"dp": (row_at * 2 + col_at) * 2 + core_at}

    around = [peer(row, col, 1 - core), peer(row, 1 - col, core)]
    around += [peer(lax.rem(row + hop, depths), col, core) for hop in range(1, depths)]

    barrier = pltpu.get_barrier_semaphore()
    for target in around:
        pl.semaphore_signal(barrier, inc=1, device_id=target, device_id_type=MESH)

    @pl.when(sends_on)
    def _():
        pl.semaphore_signal(barrier, inc=1, device_id={"layer": section - 1}, device_id_type=MESH)

    @pl.when(not_last)
    def _():
        pl.semaphore_signal(barrier, inc=1, device_id={"layer": section + 1}, device_id_type=MESH)

    def load_w(l):
        return pltpu.make_async_copy(weights.at[l], w_in.at[l], w_sem.at[l])

    def load_x(l, i):
        return pltpu.make_async_copy(states.at[l, i], x_in.at[l, i], x_sem.at[l, i])

    def load_g(i):
        return pltpu.make_async_copy(guesses.at[0, i], g_in.at[i], g_sem.at[i])

    for l in reversed(range(depth)):
        load_w(l).start()
        load_x(l, 0).start()
        if l == depth - 1:
            load_g(0).start()
    for i in range(1, images):
        for l in reversed(range(depth)):
            load_x(l, i).start()
        load_g(i).start()

    edge = jnp.zeros((width, 3 * ch), jnp.bfloat16)
    for l in range(depth):
        for i in range(images):
            for field in (x3, s3):
                field[l, i, 0, 0] = edge
                field[l, i, pairs, 1] = edge

    @pl.when(is_last)
    def _():
        corr[...] = jnp.zeros_like(corr)

    bacc[...] = jnp.zeros_like(bacc)

    @pl.loop(0, depth)
    def _(t):
        l = depth - 1 - t
        load_w(l).wait()
        wf[l, 0 : 9 * ch, 0:ch] = w_in[l]
        wf[l, 9 * ch : 12 * ch, 0:ch] = jnp.zeros((3 * ch, ch), jnp.bfloat16)
        wf[l, 0 : 3 * ch, ch : 2 * ch] = jnp.zeros((3 * ch, ch), jnp.bfloat16)
        wf[l, 3 * ch : 12 * ch, ch : 2 * ch] = w_in[l]
        for tap in range(9):
            turned = w_in[l, tap * ch : (tap + 1) * ch, :].T
            dy, dx = 2 - tap // 3, 2 - tap % 3
            for j in range(2):
                at = ((dy + j) * 3 + dx) * ch
                wt[l, at : at + ch, j * ch : (j + 1) * ch] = turned
        wt[l, 9 * ch : 12 * ch, 0:ch] = jnp.zeros((3 * ch, ch), jnp.bfloat16)
        wt[l, 0 : 3 * ch, ch : 2 * ch] = jnp.zeros((3 * ch, ch), jnp.bfloat16)

    column = lax.broadcasted_iota(jnp.int32, (1, width, ch), 1)
    leftmost, rightmost = column == 0, column == width - 1

    def chunks(lo, hi):
        return [slice(q, min(q + 4, hi)) for q in range(lo, hi, 4)]

    def spread(field, l, i, j, q, value):
        left = jnp.where(leftmost, 0.0, pltpu.roll(value, 1, 1))
        right = jnp.where(rightmost, 0.0, pltpu.roll(value, width - 1, 1))
        at = slice(q.start + j, q.stop + j)
        field[l, i, at, 1 - j, :, 0:ch] = left.astype(jnp.bfloat16)
        field[l, i, at, 1 - j, :, ch : 2 * ch] = value.astype(jnp.bfloat16)
        field[l, i, at, 1 - j, :, 2 * ch : 3 * ch] = right.astype(jnp.bfloat16)

    def windows(field, l, i, lo, hi):
        parts = [field[l, i, pl.ds(lo + r // 2, hi - lo), r % 2] for r in range(4)]
        return jnp.concatenate(parts, axis=-1).reshape((hi - lo) * width, 12 * ch)

    def product(field, kernels, l, i, lo, hi):
        out = lax.dot_general(
            windows(field, l, i, lo, hi),
            kernels[l],
            (((1,), (0,)), ((), ())),
            preferred_element_type=jnp.float32,
        )
        for q in chunks(lo, hi):
            for j in range(2):
                at = slice((q.start - lo) * width, (q.stop - lo) * width)
                yield q, j, out[at, j * ch : (j + 1) * ch].reshape(q.stop - q.start, width, ch)

    def field_step(l, i, lo, hi):
        for q in chunks(lo, hi):
            for j in range(2):
                spread(x3, l, i, j, q, x_in[l, i, q, j].astype(jnp.float32))

    def slope_step(l, i, lo, hi):
        offset = bias[pl.ds(l, 1), :].reshape(1, 1, ch)
        for q, j, part in product(x3, wf, l, i, lo, hi):
            value = jnp.tanh(part + offset)
            slope[l, i, q, j] = 1.0 - value * value

    def scale_step(l, i, lo, hi):
        for q in chunks(lo, hi):
            for j in range(2):
                spread(s3, l, i, j, q, slope[l, i, q, j] * adj[i, q, j])

    def adjoint_step(l, i, lo, hi):
        for q, j, part in product(s3, wt, l, i, lo, hi):
            adj[i, q, j] = adj[i, q, j] + step_size * part

    def turn_step(l, i):
        flat = [x3[l, i, pl.ds(j, pairs), 1 - j].reshape(pairs * width, 3 * ch) for j in range(2)]
        for j in range(2):
            xt[l, i, :, j * pairs * width : (j + 1) * pairs * width] = flat[j].T

    def grad_step(l, i, first):
        rows = []
        for j in range(2):
            parts = []
            for dy in range(3):
                r = j + 2 - dy
                parts.append(s3[l, i, pl.ds(r // 2, pairs), r % 2, :, ch : 2 * ch])
            rows.append(jnp.concatenate(parts, axis=-1).reshape(pairs * width, 3 * ch))
        right = jnp.concatenate(rows, axis=0)
        out = lax.dot_general(
            xt[l, i], right, (((1,), (0,)), ((), ())), preferred_element_type=jnp.float32
        )
        total = jnp.sum(right[:, ch : 2 * ch].astype(jnp.float32), axis=0, keepdims=True)
        bacc[pl.ds(l, 1), :] = bacc[pl.ds(l, 1), :] + total
        for dy in range(3):
            at = slice(dy * 3 * ch, (dy + 1) * 3 * ch)
            part = out[:, dy * ch : (dy + 1) * ch]
            wacc[l, at, :] = part if first else wacc[l, at, :] + part

    pieces = 4
    piece = pairs // pieces

    def message(i, at):
        return pltpu.make_async_remote_copy(
            src_ref=msg.at[i, pl.ds(at * piece, piece)],
            dst_ref=got.at[i, pl.ds(at * piece, piece)],
            send_sem=m_send.at[i, at],
            recv_sem=m_recv.at[i, at],
            device_id={"layer": section - 1},
            device_id_type=MESH,
        )

    def height(l):
        return padded if l else g.shape[4]

    def span(l, part):
        cut = round_up(padded // 2, 8)
        return slice(cut, height(l)) if part else slice(0, cut)

    def swap_cores(l, part):
        return pltpu.make_async_remote_copy(
            src_ref=g.at[l, 1 - core, :, :, span(l, part)],
            dst_ref=r1.at[l, :, :, span(l, part)],
            send_sem=send1.at[l, part],
            recv_sem=recv1.at[l, part],
            device_id=around[0],
            device_id_type=MESH,
        )

    def swap_cols(l, part):
        return pltpu.make_async_remote_copy(
            src_ref=h.at[l, 1 - col, :, span(l, part)],
            dst_ref=r2.at[l, :, span(l, part)],
            send_sem=send2.at[l, part],
            recv_sem=recv2.at[l, part],
            device_id=around[1],
            device_id_type=MESH,
        )

    def swap_rows(l, part, hop):
        return pltpu.make_async_remote_copy(
            src_ref=k.at[l, lax.rem(row + hop, depths), span(l, part)],
            dst_ref=r3.at[l, hop - 1, span(l, part)],
            send_sem=send3.at[l, part, hop - 1],
            recv_sem=recv3.at[l, part, hop - 1],
            device_id=around[1 + hop],
            device_id_type=MESH,
        )

    def reduce_1(l):
        for d in range(peers):
            at = (l, d % 2, (d // 2) % 2, d // 4)
            g[at + (slice(0, block),)] = wacc[l, d * block : (d + 1) * block, :]
            if l == 0:
                g[at + (slice(padded, None),)] = bacc[...]
        for part in range(2):
            swap_cores(l, part).start()

    def reduce_2(l, part):
        n = span(l, part)
        swap_cores(l, part).wait_recv()
        h[l, 1 - col, :, n] = g[l, core, 1 - col, :, n] + r1[l, 1 - col, :, n]
        swap_cols(l, part).start()
        h[l, col, :, n] = g[l, core, col, :, n] + r1[l, col, :, n]

    def reduce_3(l, part):
        n = span(l, part)
        swap_cols(l, part).wait_recv()
        k[l, :, n] = h[l, col, :, n] + r2[l, :, n]
        for hop in range(1, depths):
            swap_rows(l, part, hop).start()

    def reduce_4(l, part):
        n = span(l, part)
        total = k[l, row, n]
        for hop in range(1, depths):
            swap_rows(l, part, hop).wait_recv()
            total = total + r3[l, hop - 1, n]
        last = min(n.stop, block)
        weight_grad[l, n.start : last] = scale * total[0 : last - n.start]
        if l == 0 and part == 1:
            sums = total[padded - n.start : padded - n.start + depth]
            lane = lax.broadcasted_iota(jnp.int32, sums.shape, 1)
            share = bias_grad.shape[1]
            for at in range(share):
                mine = jnp.where(lane == me * share + at, sums, 0.0)
                bias_grad[:, at : at + 1] = scale * jnp.sum(mine, axis=1, keepdims=True)

    def all_here():
        neighbours = sends_on.astype(jnp.int32) + not_last.astype(jnp.int32)
        pl.semaphore_wait(barrier, len(around) + neighbours)

    half = pairs // 2

    def first_pass(i, band):
        def part_of(extra):
            cut = min(half + extra, pairs)
            return (cut, pairs) if band else (0, cut)

        for l in reversed(range(depth)):
            if band == 0:
                load_x(l, i).wait()
            field_step(l, i, *part_of(l + 2))
            slope_step(l, i, *part_of(l + 1))
            scale_step(l, i, *part_of(l + 1))
            adjoint_step(l, i, *part_of(l))

    def send_band(i, band):
        factor = gain[pl.ds(section - 1, 1), :].reshape(1, 1, 1, ch)
        count = pieces // 2
        for at in range(band * count, (band + 1) * count):
            rows = slice(at * piece, (at + 1) * piece)

            @pl.when(not_last)
            def _():
                message(i, at).wait_recv()
                corr[i, rows] = got[i, rows] - g_in[i, rows]

            msg[i, rows] = adj[i, rows] + factor * corr[i, rows]
            message(i, at).start()

    @pl.when(sends_on)
    def _():
        @pl.loop(0, images)
        def _(i):
            load_g(i).wait()
            adj[i] = g_in[i]
            first_pass(i, 0)

            @pl.when(i == 0)
            def _():
                all_here()

            send_band(i, 0)
            first_pass(i, 1)
            send_band(i, 1)

    @pl.when(jnp.logical_not(sends_on))
    def _():
        @pl.loop(0, images)
        def _(i):
            load_g(i).wait()

            @pl.loop(0, depth)
            def _(t):
                l = depth - 1 - t
                load_x(l, i).wait()
                field_step(l, i, 0, pairs)
                slope_step(l, i, 0, pairs)

        all_here()

    @pl.loop(0, images)
    def _(i):
        @pl.loop(0, depth)
        def _(l):
            turn_step(l, i)

    def begin(i):
        @pl.when(section == 0)
        def _():
            for at in range(pieces):
                message(i, at).wait_recv()

        @pl.when(not_last)
        def _():
            adj[i] = got[i]

    def store(i):
        return pltpu.make_async_copy(adj.at[i], starts.at[0, i], o_sem.at[i])

    for i in range(images - 1):
        begin(i)

        @pl.loop(0, depth)
        def _(t):
            l = depth - 1 - t

            @pl.when(not_last)
            def _():
                scale_step(l, i, 0, pairs)
                adjoint_step(l, i, 0, pairs)

            grad_step(l, i, i == 0)

        store(i).start()

    i = images - 1
    begin(i)
    for l in reversed(range(depth)):
        @pl.when(not_last)
        def _():
            scale_step(l, i, 0, pairs)

        grad_step(l, i, i == 0)
        reduce_1(l)

        @pl.when(not_last)
        def _():
            adjoint_step(l, i, 0, pairs)

        for part in range(2):
            reduce_2(l, part)
        if l < depth - 1:
            for part in range(2):
                reduce_3(l + 1, part)
    store(i).start()
    for part in range(2):
        reduce_3(0, part)
    for l in reversed(range(depth)):
        for part in range(2):
            reduce_4(l, part)

    for i in range(images):
        store(i).wait()

        @pl.when(sends_on)
        def _():
            for at in range(pieces):
                message(i, at).wait_send()

    for l in range(depth):
        for part in range(2):
            swap_cores(l, part).wait_send()
            swap_cols(l, part).wait_send()
            for hop in range(1, depths):
                swap_rows(l, part, hop).wait_send()


def hand_over(starts, weight_grad, bias_grad, starts_out, weight_out, bias_out, a, b, c, in_sem, out_sem):
    images, pairs = starts.shape[1:3]
    parts = 4 if pairs % 4 == 0 else 1
    some = pairs // parts
    ways = [(weight_grad, b, weight_out), (bias_grad, c, bias_out)]
    for i in range(images):
        for part in range(parts):
            at = (0, i, pl.ds(part * some, some))
            ways.append((starts.at[at], a.at[at], starts_out.at[at]))
    loads = [pltpu.make_async_copy(way[0], way[1], in_sem.at[n]) for n, way in enumerate(ways)]
    stores = [pltpu.make_async_copy(way[1], way[2], out_sem.at[n]) for n, way in enumerate(ways)]
    for load in loads:
        load.start()
    for load, store in zip(loads, stores):
        load.wait()
        store.start()
    for store in stores:
        store.wait()


def per_device(sections, peers, states, weights, bias, guesses, coarse_gain):
    depth, images, high, width, ch = states.shape
    pairs = high // 2
    rows = 9 * ch // peers
    depths = peers // 4
    tall = round_up(rows, 8) + round_up(depth, 8)
    scale = step_size / (images * peers)
    f32, bf16 = jnp.float32, jnp.bfloat16
    image = (images, pairs, 2, width, ch)
    taps = (depth, images, pairs + 1, 2, width, 3 * ch)
    dma = pltpu.SemaphoreType.DMA
    conv_flops = 2 * images * high * width * 9 * ch * ch
    vmem, anywhere = pl.BlockSpec(memory_space=pltpu.VMEM), pl.BlockSpec(memory_space=pl.ANY)
    starts, weight_grad, bias_grad = pl.pallas_call(
        functools.partial(kernel, sections, peers, scale),
        out_shape=(
            jax.ShapeDtypeStruct((1,) + image, f32),
            jax.ShapeDtypeStruct((depth, rows, ch), f32),
            jax.ShapeDtypeStruct((depth, ch // peers), f32),
        ),
        in_specs=[anywhere, anywhere, vmem, anywhere, vmem],
        out_specs=(anywhere, vmem, vmem),
        scratch_shapes=[
            pltpu.VMEM((depth,) + image, bf16),
            pltpu.VMEM((depth, 9 * ch, ch), bf16),
            pltpu.VMEM(image, f32),
            pltpu.VMEM((depth, 12 * ch, 2 * ch), bf16),
            pltpu.VMEM((depth, 12 * ch, 2 * ch), bf16),
            pltpu.VMEM(taps, bf16),
            pltpu.VMEM((depth, images, 3 * ch, high * width), bf16),
            pltpu.VMEM((depth,) + image, f32),
            pltpu.VMEM(taps, bf16),
            pltpu.VMEM(image, f32),
            pltpu.VMEM(image, f32),
            pltpu.VMEM(image, f32),
            pltpu.VMEM(image, f32),
            pltpu.VMEM((depth, 9 * ch, ch), f32),
            pltpu.VMEM((round_up(depth, 8), ch), f32),
            pltpu.VMEM((depth, 2, 2, depths, tall, ch), f32),
            pltpu.VMEM((depth, 2, depths, tall, ch), f32),
            pltpu.VMEM((depth, 2, depths, tall, ch), f32),
            pltpu.VMEM((depth, depths, tall, ch), f32),
            pltpu.VMEM((depth, depths, tall, ch), f32),
            pltpu.VMEM((depth, depths, tall, ch), f32),
            dma((depth,)), dma((depth, images)), dma((images,)), dma((images,)),
            dma((images, 4)), dma((images, 4)),
            dma((depth, 2)), dma((depth, 2)), dma((depth, 2)), dma((depth, 2)),
            dma((depth, 2, depths)), dma((depth, 2, depths)),
        ],
        compiler_params=pltpu.CompilerParams(
            collective_id=0, has_side_effects=True, vmem_limit_bytes=56 * 1024 * 1024
        ),
        cost_estimate=pl.CostEstimate(
            flops=9 * conv_flops, bytes_accessed=8 * states.size, transcendentals=states.size
        ),
    )(
        states.reshape((depth,) + image),
        weights,
        bias,
        guesses.reshape((1,) + image),
        coarse_gain,
    )
    starts, weight_grad, bias_grad = pl.pallas_call(
        hand_over,
        out_shape=(
            jax.ShapeDtypeStruct(starts.shape, f32),
            jax.ShapeDtypeStruct(weight_grad.shape, f32),
            jax.ShapeDtypeStruct(bias_grad.shape, f32),
        ),
        in_specs=[anywhere] * 3,
        out_specs=(anywhere,) * 3,
        scratch_shapes=[
            pltpu.VMEM(starts.shape, f32),
            pltpu.VMEM(weight_grad.shape, f32),
            pltpu.VMEM(bias_grad.shape, f32),
            dma((images * 4 + 2,)),
            dma((images * 4 + 2,)),
        ],
        compiler_params=pltpu.CompilerParams(vmem_limit_bytes=60 * 1024 * 1024),
    )(starts, weight_grad, bias_grad)
    return starts.reshape(guesses.shape), weight_grad, bias_grad


def solution(mesh):
    return jax.shard_map(
        functools.partial(per_device, mesh.shape["layer"], mesh.shape["dp"]),
        mesh=mesh,
        in_specs=(
            P("layer", "dp", None, None, None),
            P("layer", None, None),
            P("layer", None),
            P("layer", "dp", None, None, None),
            P(),
        ),
        out_specs=(P("layer", "dp", None, None, None), P("layer", "dp", None), P("layer", "dp")),
        check_vma=False,
    )
```

```python
import functools

import jax
import jax.numpy as jnp
from jax import lax
from jax.experimental import pallas as pl
from jax.experimental.pallas import tpu as pltpu
from jax.sharding import PartitionSpec as P

MESH = pl.DeviceIdType.MESH
step_size = 0.5


def round_up(value, multiple):
    return -(-value // multiple) * multiple


def kernel(
    sections, peers, scale,
    states, weights, bias, guesses, gain,
    starts, weight_grad, bias_grad,
    x_in, w_in, g_in, wf, wt, x3, xt, slope, s3, adj, corr, msg, got, wacc, bacc,
    g, r1, h, r2, k, r3,
    w_sem, x_sem, g_sem, o_sem, m_send, m_recv,
    send1, recv1, send2, recv2, send3, recv3,
):
    depth, images, pairs, _, width, ch = states.shape
    depths = peers // 4
    block = weight_grad.shape[1]
    padded = round_up(block, 8)
    section = lax.axis_index("layer")
    me = lax.axis_index("dp")
    core = lax.rem(me, 2)
    col = lax.rem(lax.div(me, 2), 2)
    row = lax.div(me, 4)
    is_last = section == sections - 1
    not_last = section < sections - 1
    sends_on = section > 0

    def peer(row_at, col_at, core_at):
        return {"dp": (row_at * 2 + col_at) * 2 + core_at}

    around = [peer(row, col, 1 - core), peer(row, 1 - col, core)]
    around += [peer(lax.rem(row + hop, depths), col, core) for hop in range(1, depths)]

    barrier = pltpu.get_barrier_semaphore()
    for target in around:
        pl.semaphore_signal(barrier, inc=1, device_id=target, device_id_type=MESH)

    @pl.when(sends_on)
    def _():
        pl.semaphore_signal(barrier, inc=1, device_id={"layer": section - 1}, device_id_type=MESH)

    @pl.when(not_last)
    def _():
        pl.semaphore_signal(barrier, inc=1, device_id={"layer": section + 1}, device_id_type=MESH)

    def load_w(l):
        return pltpu.make_async_copy(weights.at[l], w_in.at[l], w_sem.at[l])

    def load_x(l, i):
        return pltpu.make_async_copy(states.at[l, i], x_in.at[l, i], x_sem.at[l, i])

    def load_g(i):
        return pltpu.make_async_copy(guesses.at[0, i], g_in.at[i], g_sem.at[i])

    for l in reversed(range(depth)):
        load_w(l).start()
        load_x(l, 0).start()
        if l == depth - 1:
            load_g(0).start()
    for i in range(1, images):
        for l in reversed(range(depth)):
            load_x(l, i).start()
        load_g(i).start()

    edge = jnp.zeros((width, 3 * ch), jnp.bfloat16)
    for l in range(depth):
        for i in range(images):
            for field in (x3, s3):
                field[l, i, 0, 0] = edge
                field[l, i, pairs, 1] = edge

    @pl.when(is_last)
    def _():
        corr[...] = jnp.zeros_like(corr)

    bacc[...] = jnp.zeros_like(bacc)

    def prepare(l):
        load_w(l).wait()
        wf[l, 0 : 9 * ch, 0:ch] = w_in[l]
        wf[l, 9 * ch : 12 * ch, 0:ch] = jnp.zeros((3 * ch, ch), jnp.bfloat16)
        wf[l, 0 : 3 * ch, ch : 2 * ch] = jnp.zeros((3 * ch, ch), jnp.bfloat16)
        wf[l, 3 * ch : 12 * ch, ch : 2 * ch] = w_in[l]
        for tap in range(9):
            turned = w_in[l, tap * ch : (tap + 1) * ch, :].T
            dy, dx = 2 - tap // 3, 2 - tap % 3
            for j in range(2):
                at = ((dy + j) * 3 + dx) * ch
                wt[l, at : at + ch, j * ch : (j + 1) * ch] = turned
        wt[l, 9 * ch : 12 * ch, 0:ch] = jnp.zeros((3 * ch, ch), jnp.bfloat16)
        wt[l, 0 : 3 * ch, ch : 2 * ch] = jnp.zeros((3 * ch, ch), jnp.bfloat16)

    column = lax.broadcasted_iota(jnp.int32, (1, width, ch), 1)
    leftmost, rightmost = column == 0, column == width - 1

    def chunks(lo, hi):
        return [slice(q, min(q + 4, hi)) for q in range(lo, hi, 4)]

    def spread(field, l, i, j, q, value):
        left = jnp.where(leftmost, 0.0, pltpu.roll(value, 1, 1))
        right = jnp.where(rightmost, 0.0, pltpu.roll(value, width - 1, 1))
        at = slice(q.start + j, q.stop + j)
        field[l, i, at, 1 - j, :, 0:ch] = left.astype(jnp.bfloat16)
        field[l, i, at, 1 - j, :, ch : 2 * ch] = value.astype(jnp.bfloat16)
        field[l, i, at, 1 - j, :, 2 * ch : 3 * ch] = right.astype(jnp.bfloat16)

    def windows(field, l, i, lo, hi):
        parts = [field[l, i, pl.ds(lo + r // 2, hi - lo), r % 2] for r in range(4)]
        return jnp.concatenate(parts, axis=-1).reshape((hi - lo) * width, 12 * ch)

    def product(field, kernels, l, i, lo, hi):
        out = lax.dot_general(
            windows(field, l, i, lo, hi),
            kernels[l],
            (((1,), (0,)), ((), ())),
            preferred_element_type=jnp.float32,
        )
        for q in chunks(lo, hi):
            for j in range(2):
                at = slice((q.start - lo) * width, (q.stop - lo) * width)
                yield q, j, out[at, j * ch : (j + 1) * ch].reshape(q.stop - q.start, width, ch)

    def field_step(l, i, lo, hi):
        for q in chunks(lo, hi):
            for j in range(2):
                spread(x3, l, i, j, q, x_in[l, i, q, j].astype(jnp.float32))

    def slope_step(l, i, lo, hi):
        offset = bias[pl.ds(l, 1), :].reshape(1, 1, ch)
        for q, j, part in product(x3, wf, l, i, lo, hi):
            value = jnp.tanh(part + offset)
            slope[l, i, q, j] = 1.0 - value * value

    def scale_step(l, i, lo, hi):
        for q in chunks(lo, hi):
            for j in range(2):
                spread(s3, l, i, j, q, slope[l, i, q, j] * adj[i, q, j])

    def adjoint_step(l, i, lo, hi):
        for q, j, part in product(s3, wt, l, i, lo, hi):
            adj[i, q, j] = adj[i, q, j] + step_size * part

    def turn_step(l, i):
        flat = [x3[l, i, pl.ds(j, pairs), 1 - j].reshape(pairs * width, 3 * ch) for j in range(2)]
        for j in range(2):
            xt[l, i, :, j * pairs * width : (j + 1) * pairs * width] = flat[j].T

    def grad_step(l, i, first):
        rows = []
        for j in range(2):
            parts = []
            for dy in range(3):
                r = j + 2 - dy
                parts.append(s3[l, i, pl.ds(r // 2, pairs), r % 2, :, ch : 2 * ch])
            rows.append(jnp.concatenate(parts, axis=-1).reshape(pairs * width, 3 * ch))
        right = jnp.concatenate(rows, axis=0)
        out = lax.dot_general(
            xt[l, i], right, (((1,), (0,)), ((), ())), preferred_element_type=jnp.float32
        )
        total = jnp.sum(right[:, ch : 2 * ch].astype(jnp.float32), axis=0, keepdims=True)
        bacc[pl.ds(l, 1), :] = bacc[pl.ds(l, 1), :] + total
        for dy in range(3):
            at = slice(dy * 3 * ch, (dy + 1) * 3 * ch)
            part = out[:, dy * ch : (dy + 1) * ch]
            wacc[l, at, :] = part if first else wacc[l, at, :] + part

    pieces = 4
    piece = pairs // pieces

    def message(i, at):
        return pltpu.make_async_remote_copy(
            src_ref=msg.at[i, pl.ds(at * piece, piece)],
            dst_ref=got.at[i, pl.ds(at * piece, piece)],
            send_sem=m_send.at[i, at],
            recv_sem=m_recv.at[i, at],
            device_id={"layer": section - 1},
            device_id_type=MESH,
        )

    def height(l):
        return padded if l else g.shape[4]

    def span(l, part):
        cut = round_up(padded // 2, 8)
        return slice(cut, height(l)) if part else slice(0, cut)

    def swap_cores(l, part):
        return pltpu.make_async_remote_copy(
            src_ref=g.at[l, 1 - core, :, :, span(l, part)],
            dst_ref=r1.at[l, :, :, span(l, part)],
            send_sem=send1.at[l, part],
            recv_sem=recv1.at[l, part],
            device_id=around[0],
            device_id_type=MESH,
        )

    def swap_cols(l, part):
        return pltpu.make_async_remote_copy(
            src_ref=h.at[l, 1 - col, :, span(l, part)],
            dst_ref=r2.at[l, :, span(l, part)],
            send_sem=send2.at[l, part],
            recv_sem=recv2.at[l, part],
            device_id=around[1],
            device_id_type=MESH,
        )

    def swap_rows(l, part, hop):
        return pltpu.make_async_remote_copy(
            src_ref=k.at[l, lax.rem(row + hop, depths), span(l, part)],
            dst_ref=r3.at[l, hop - 1, span(l, part)],
            send_sem=send3.at[l, part, hop - 1],
            recv_sem=recv3.at[l, part, hop - 1],
            device_id=around[1 + hop],
            device_id_type=MESH,
        )

    def reduce_1(l):
        for d in range(peers):
            at = (l, d % 2, (d // 2) % 2, d // 4)
            g[at + (slice(0, block),)] = wacc[l, d * block : (d + 1) * block, :]
            if l == 0:
                g[at + (slice(padded, None),)] = bacc[...]
        for part in range(2):
            swap_cores(l, part).start()

    def reduce_2(l, part):
        n = span(l, part)
        swap_cores(l, part).wait_recv()
        h[l, 1 - col, :, n] = g[l, core, 1 - col, :, n] + r1[l, 1 - col, :, n]
        swap_cols(l, part).start()
        h[l, col, :, n] = g[l, core, col, :, n] + r1[l, col, :, n]

    def reduce_3(l, part):
        n = span(l, part)
        swap_cols(l, part).wait_recv()
        k[l, :, n] = h[l, col, :, n] + r2[l, :, n]
        for hop in range(1, depths):
            swap_rows(l, part, hop).start()

    def reduce_4(l, part):
        n = span(l, part)
        total = k[l, row, n]
        for hop in range(1, depths):
            swap_rows(l, part, hop).wait_recv()
            total = total + r3[l, hop - 1, n]
        last = min(n.stop, block)
        weight_grad[l, n.start : last] = scale * total[0 : last - n.start]
        if l == 0 and part == 1:
            sums = total[padded - n.start : padded - n.start + depth]
            lane = lax.broadcasted_iota(jnp.int32, sums.shape, 1)
            share = bias_grad.shape[1]
            for at in range(share):
                mine = jnp.where(lane == me * share + at, sums, 0.0)
                bias_grad[:, at : at + 1] = scale * jnp.sum(mine, axis=1, keepdims=True)

    def all_here():
        neighbours = sends_on.astype(jnp.int32) + not_last.astype(jnp.int32)
        pl.semaphore_wait(barrier, len(around) + neighbours)

    def first_pass(i, start, stop, prepares):
        def span_of(extra):
            return min(start + extra, pairs) if start else 0, min(stop + extra, pairs)

        for l in reversed(range(depth)):
            if prepares:
                prepare(l)
            if start == 0:
                load_x(l, i).wait()
            field_step(l, i, *span_of(l + 2))
            slope_step(l, i, *span_of(l + 1))
            scale_step(l, i, *span_of(l + 1))
            adjoint_step(l, i, *span_of(l))

    def send_band(i, start, stop):
        factor = gain[pl.ds(section - 1, 1), :].reshape(1, 1, 1, ch)
        for at in range(start // piece, stop // piece):
            rows = slice(at * piece, (at + 1) * piece)

            @pl.when(not_last)
            def _():
                message(i, at).wait_recv()
                corr[i, rows] = got[i, rows] - g_in[i, rows]

            msg[i, rows] = adj[i, rows] + factor * corr[i, rows]
            message(i, at).start()

    @pl.when(sends_on)
    def _():
        load_g(0).wait()
        adj[0] = g_in[0]
        bands = [(0, piece), (piece, 2 * piece), (2 * piece, pairs)]
        for start, stop in bands:
            first_pass(0, start, stop, start == 0)
            if start == 0:
                all_here()
            send_band(0, start, stop)

        @pl.loop(1, images)
        def _(i):
            load_g(i).wait()
            adj[i] = g_in[i]
            for start, stop in ((0, 2 * piece), (2 * piece, pairs)):
                first_pass(i, start, stop, False)
                send_band(i, start, stop)

    @pl.when(jnp.logical_not(sends_on))
    def _():
        @pl.loop(0, depth)
        def _(l):
            prepare(l)

        @pl.loop(0, images)
        def _(i):
            load_g(i).wait()

            @pl.loop(0, depth)
            def _(t):
                l = depth - 1 - t
                load_x(l, i).wait()
                field_step(l, i, 0, pairs)
                slope_step(l, i, 0, pairs)

        all_here()

    @pl.loop(0, images)
    def _(i):
        @pl.loop(0, depth)
        def _(l):
            turn_step(l, i)

    def begin(i, start, stop):
        @pl.when(section == 0)
        def _():
            for at in range(start // piece, stop // piece):
                message(i, at).wait_recv()

        @pl.when(not_last)
        def _():
            adj[i, start:stop] = got[i, start:stop]

    def store(i):
        return pltpu.make_async_copy(adj.at[i], starts.at[0, i], o_sem.at[i])

    for i in range(images - 1):
        begin(i, 0, pairs)

        @pl.loop(0, depth)
        def _(t):
            l = depth - 1 - t

            @pl.when(not_last)
            def _():
                scale_step(l, i, 0, pairs)
                adjoint_step(l, i, 0, pairs)

            grad_step(l, i, i == 0)

        store(i).start()

    i = images - 1
    for start, stop in ((0, 3 * piece), (3 * piece, pairs)):
        begin(i, start, stop)

        @pl.when(not_last)
        def _():
            scale_step(depth - 1, i, start, stop)

    for l in reversed(range(depth)):
        if l < depth - 1:
            @pl.when(not_last)
            def _():
                scale_step(l, i, 0, pairs)

        grad_step(l, i, i == 0)
        reduce_1(l)

        @pl.when(not_last)
        def _():
            adjoint_step(l, i, 0, pairs)

        for part in range(2):
            reduce_2(l, part)
        if l < depth - 1:
            for part in range(2):
                reduce_3(l + 1, part)
    store(i).start()
    for part in range(2):
        reduce_3(0, part)
    for l in reversed(range(depth)):
        for part in range(2):
            reduce_4(l, part)

    for i in range(images):
        store(i).wait()

        @pl.when(sends_on)
        def _():
            for at in range(pieces):
                message(i, at).wait_send()

    for l in range(depth):
        for part in range(2):
            swap_cores(l, part).wait_send()
            swap_cols(l, part).wait_send()
            for hop in range(1, depths):
                swap_rows(l, part, hop).wait_send()


def hand_over(starts, weight_grad, bias_grad, starts_out, weight_out, bias_out, a, b, c, in_sem, out_sem):
    images, pairs = starts.shape[1:3]
    parts = 4 if pairs % 4 == 0 else 1
    some = pairs // parts
    ways = [(weight_grad, b, weight_out), (bias_grad, c, bias_out)]
    for i in range(images):
        for part in range(parts):
            at = (0, i, pl.ds(part * some, some))
            ways.append((starts.at[at], a.at[at], starts_out.at[at]))
    loads = [pltpu.make_async_copy(way[0], way[1], in_sem.at[n]) for n, way in enumerate(ways)]
    stores = [pltpu.make_async_copy(way[1], way[2], out_sem.at[n]) for n, way in enumerate(ways)]
    for load in loads:
        load.start()
    for load, store in zip(loads, stores):
        load.wait()
        store.start()
    for store in stores:
        store.wait()


def per_device(sections, peers, states, weights, bias, guesses, coarse_gain):
    depth, images, high, width, ch = states.shape
    pairs = high // 2
    rows = 9 * ch // peers
    depths = peers // 4
    tall = round_up(rows, 8) + round_up(depth, 8)
    scale = step_size / (images * peers)
    f32, bf16 = jnp.float32, jnp.bfloat16
    image = (images, pairs, 2, width, ch)
    taps = (depth, images, pairs + 1, 2, width, 3 * ch)
    dma = pltpu.SemaphoreType.DMA
    conv_flops = 2 * images * high * width * 9 * ch * ch
    vmem, anywhere = pl.BlockSpec(memory_space=pltpu.VMEM), pl.BlockSpec(memory_space=pl.ANY)
    starts, weight_grad, bias_grad = pl.pallas_call(
        functools.partial(kernel, sections, peers, scale),
        out_shape=(
            jax.ShapeDtypeStruct((1,) + image, f32),
            jax.ShapeDtypeStruct((depth, rows, ch), f32),
            jax.ShapeDtypeStruct((depth, ch // peers), f32),
        ),
        in_specs=[anywhere, anywhere, vmem, anywhere, vmem],
        out_specs=(anywhere, vmem, vmem),
        scratch_shapes=[
            pltpu.VMEM((depth,) + image, bf16),
            pltpu.VMEM((depth, 9 * ch, ch), bf16),
            pltpu.VMEM(image, f32),
            pltpu.VMEM((depth, 12 * ch, 2 * ch), bf16),
            pltpu.VMEM((depth, 12 * ch, 2 * ch), bf16),
            pltpu.VMEM(taps, bf16),
            pltpu.VMEM((depth, images, 3 * ch, high * width), bf16),
            pltpu.VMEM((depth,) + image, f32),
            pltpu.VMEM(taps, bf16),
            pltpu.VMEM(image, f32),
            pltpu.VMEM(image, f32),
            pltpu.VMEM(image, f32),
            pltpu.VMEM(image, f32),
            pltpu.VMEM((depth, 9 * ch, ch), f32),
            pltpu.VMEM((round_up(depth, 8), ch), f32),
            pltpu.VMEM((depth, 2, 2, depths, tall, ch), f32),
            pltpu.VMEM((depth, 2, depths, tall, ch), f32),
            pltpu.VMEM((depth, 2, depths, tall, ch), f32),
            pltpu.VMEM((depth, depths, tall, ch), f32),
            pltpu.VMEM((depth, depths, tall, ch), f32),
            pltpu.VMEM((depth, depths, tall, ch), f32),
            dma((depth,)), dma((depth, images)), dma((images,)), dma((images,)),
            dma((images, 4)), dma((images, 4)),
            dma((depth, 2)), dma((depth, 2)), dma((depth, 2)), dma((depth, 2)),
            dma((depth, 2, depths)), dma((depth, 2, depths)),
        ],
        compiler_params=pltpu.CompilerParams(
            collective_id=0, has_side_effects=True, vmem_limit_bytes=56 * 1024 * 1024
        ),
        cost_estimate=pl.CostEstimate(
            flops=9 * conv_flops, bytes_accessed=8 * states.size, transcendentals=states.size
        ),
    )(
        states.reshape((depth,) + image),
        weights,
        bias,
        guesses.reshape((1,) + image),
        coarse_gain,
    )
    starts, weight_grad, bias_grad = pl.pallas_call(
        hand_over,
        out_shape=(
            jax.ShapeDtypeStruct(starts.shape, f32),
            jax.ShapeDtypeStruct(weight_grad.shape, f32),
            jax.ShapeDtypeStruct(bias_grad.shape, f32),
        ),
        in_specs=[anywhere] * 3,
        out_specs=(anywhere,) * 3,
        scratch_shapes=[
            pltpu.VMEM(starts.shape, f32),
            pltpu.VMEM(weight_grad.shape, f32),
            pltpu.VMEM(bias_grad.shape, f32),
            dma((images * 4 + 2,)),
            dma((images * 4 + 2,)),
        ],
        compiler_params=pltpu.CompilerParams(vmem_limit_bytes=60 * 1024 * 1024),
    )(starts, weight_grad, bias_grad)
    return starts.reshape(guesses.shape), weight_grad, bias_grad


def solution(mesh):
    return jax.shard_map(
        functools.partial(per_device, mesh.shape["layer"], mesh.shape["dp"]),
        mesh=mesh,
        in_specs=(
            P("layer", "dp", None, None, None),
            P("layer", None, None),
            P("layer", None),
            P("layer", "dp", None, None, None),
            P(),
        ),
        out_specs=(P("layer", "dp", None, None, None), P("layer", "dp", None), P("layer", "dp")),
        check_vma=False,
    )
```

```python
import functools

import jax
import jax.numpy as jnp
from jax import lax
from jax.experimental import pallas as pl
from jax.experimental.pallas import tpu as pltpu
from jax.sharding import PartitionSpec as P

MESH = pl.DeviceIdType.MESH
step_size = 0.5


def round_up(value, multiple):
    return -(-value // multiple) * multiple


def kernel(
    sections, peers, scale,
    states, weights, bias, guesses, gain,
    starts, weight_grad, bias_grad,
    x_in, w_in, g_in, wf, wt, x3, xt, slope, s3, adj, corr, msg, got, wacc, bacc,
    g, r1, h, r2, k, r3,
    w_sem, x_sem, g_sem, o_sem, m_send, m_recv,
    send1, recv1, send2, recv2, send3, recv3,
):
    depth, images, pairs, _, width, ch = states.shape
    depths = peers // 4
    block = weight_grad.shape[1]
    padded = round_up(block, 8)
    section = lax.axis_index("layer")
    me = lax.axis_index("dp")
    core = lax.rem(me, 2)
    col = lax.rem(lax.div(me, 2), 2)
    row = lax.div(me, 4)
    is_last = section == sections - 1
    not_last = section < sections - 1
    sends_on = section > 0

    def peer(row_at, col_at, core_at):
        return {"dp": (row_at * 2 + col_at) * 2 + core_at}

    around = [peer(row, col, 1 - core), peer(row, 1 - col, core)]
    around += [peer(lax.rem(row + hop, depths), col, core) for hop in range(1, depths)]

    def load_w(l):
        return pltpu.make_async_copy(weights.at[l], w_in.at[l], w_sem.at[l])

    def load_x(l, i):
        return pltpu.make_async_copy(states.at[l, i], x_in.at[l, i], x_sem.at[l, i])

    def load_g(i):
        return pltpu.make_async_copy(guesses.at[0, i], g_in.at[i], g_sem.at[i])

    for l in reversed(range(depth)):
        load_w(l).start()
        load_x(l, 0).start()
        if l == depth - 1:
            load_g(0).start()
    for i in range(1, images):
        for l in reversed(range(depth)):
            load_x(l, i).start()
        load_g(i).start()

    barrier = pltpu.get_barrier_semaphore()
    for target in around:
        pl.semaphore_signal(barrier, inc=1, device_id=target, device_id_type=MESH)

    @pl.when(sends_on)
    def _():
        pl.semaphore_signal(barrier, inc=1, device_id={"layer": section - 1}, device_id_type=MESH)

    @pl.when(not_last)
    def _():
        pl.semaphore_signal(barrier, inc=1, device_id={"layer": section + 1}, device_id_type=MESH)

    edge = jnp.zeros((width, 3 * ch), jnp.bfloat16)
    for l in range(depth):
        for i in range(images):
            for field in (x3, s3):
                field[l, i, 0, 0] = edge
                field[l, i, pairs, 1] = edge

    @pl.when(is_last)
    def _():
        corr[...] = jnp.zeros_like(corr)

    bacc[...] = jnp.zeros_like(bacc)

    def prepare(l):
        load_w(l).wait()
        wf[l, 0 : 9 * ch, 0:ch] = w_in[l]
        wf[l, 9 * ch : 12 * ch, 0:ch] = jnp.zeros((3 * ch, ch), jnp.bfloat16)
        wf[l, 0 : 3 * ch, ch : 2 * ch] = jnp.zeros((3 * ch, ch), jnp.bfloat16)
        wf[l, 3 * ch : 12 * ch, ch : 2 * ch] = w_in[l]
        for tap in range(9):
            turned = w_in[l, tap * ch : (tap + 1) * ch, :].T
            dy, dx = 2 - tap // 3, 2 - tap % 3
            for j in range(2):
                at = ((dy + j) * 3 + dx) * ch
                wt[l, at : at + ch, j * ch : (j + 1) * ch] = turned
        wt[l, 9 * ch : 12 * ch, 0:ch] = jnp.zeros((3 * ch, ch), jnp.bfloat16)
        wt[l, 0 : 3 * ch, ch : 2 * ch] = jnp.zeros((3 * ch, ch), jnp.bfloat16)

    column = lax.broadcasted_iota(jnp.int32, (1, width, ch), 1)
    leftmost, rightmost = column == 0, column == width - 1

    def chunks(lo, hi):
        return [slice(q, min(q + 4, hi)) for q in range(lo, hi, 4)]

    def spread(field, l, i, j, q, value):
        left = jnp.where(leftmost, 0.0, pltpu.roll(value, 1, 1))
        right = jnp.where(rightmost, 0.0, pltpu.roll(value, width - 1, 1))
        at = slice(q.start + j, q.stop + j)
        field[l, i, at, 1 - j, :, 0:ch] = left.astype(jnp.bfloat16)
        field[l, i, at, 1 - j, :, ch : 2 * ch] = value.astype(jnp.bfloat16)
        field[l, i, at, 1 - j, :, 2 * ch : 3 * ch] = right.astype(jnp.bfloat16)

    def windows(field, l, i, lo, hi):
        parts = [field[l, i, pl.ds(lo + r // 2, hi - lo), r % 2] for r in range(4)]
        return jnp.concatenate(parts, axis=-1).reshape((hi - lo) * width, 12 * ch)

    def product(field, kernels, l, i, lo, hi):
        out = lax.dot_general(
            windows(field, l, i, lo, hi),
            kernels[l],
            (((1,), (0,)), ((), ())),
            preferred_element_type=jnp.float32,
        )
        for q in chunks(lo, hi):
            for j in range(2):
                at = slice((q.start - lo) * width, (q.stop - lo) * width)
                yield q, j, out[at, j * ch : (j + 1) * ch].reshape(q.stop - q.start, width, ch)

    def field_step(l, i, lo, hi):
        for q in chunks(lo, hi):
            for j in range(2):
                spread(x3, l, i, j, q, x_in[l, i, q, j].astype(jnp.float32))

    def slope_step(l, i, lo, hi):
        offset = bias[pl.ds(l, 1), :].reshape(1, 1, ch)
        for q, j, part in product(x3, wf, l, i, lo, hi):
            value = jnp.tanh(part + offset)
            slope[l, i, q, j] = 1.0 - value * value

    def scale_step(l, i, lo, hi):
        for q in chunks(lo, hi):
            for j in range(2):
                spread(s3, l, i, j, q, slope[l, i, q, j] * adj[i, q, j])

    def adjoint_step(l, i, lo, hi):
        for q, j, part in product(s3, wt, l, i, lo, hi):
            adj[i, q, j] = adj[i, q, j] + step_size * part

    def turn_step(l, i):
        flat = [x3[l, i, pl.ds(j, pairs), 1 - j].reshape(pairs * width, 3 * ch) for j in range(2)]
        for j in range(2):
            xt[l, i, :, j * pairs * width : (j + 1) * pairs * width] = flat[j].T

    def grad_step(l, i, lo, hi, first):
        rows, left = [], []
        for j in range(2):
            parts = []
            for dy in range(3):
                r = j + 2 - dy
                parts.append(s3[l, i, pl.ds(lo + r // 2, hi - lo), r % 2, :, ch : 2 * ch])
            rows.append(jnp.concatenate(parts, axis=-1).reshape((hi - lo) * width, 3 * ch))
            left.append(xt[l, i, :, (j * pairs + lo) * width : (j * pairs + hi) * width])
        right = jnp.concatenate(rows, axis=0)
        out = lax.dot_general(
            jnp.concatenate(left, axis=1),
            right,
            (((1,), (0,)), ((), ())),
            preferred_element_type=jnp.float32,
        )
        total = jnp.sum(right[:, ch : 2 * ch].astype(jnp.float32), axis=0, keepdims=True)
        bacc[pl.ds(l, 1), :] = bacc[pl.ds(l, 1), :] + total
        for dy in range(3):
            at = slice(dy * 3 * ch, (dy + 1) * 3 * ch)
            part = out[:, dy * ch : (dy + 1) * ch]
            wacc[l, at, :] = part if first else wacc[l, at, :] + part

    pieces = 4
    piece = pairs // pieces

    def message(i, at):
        return pltpu.make_async_remote_copy(
            src_ref=msg.at[i, pl.ds(at * piece, piece)],
            dst_ref=got.at[i, pl.ds(at * piece, piece)],
            send_sem=m_send.at[i, at],
            recv_sem=m_recv.at[i, at],
            device_id={"layer": section - 1},
            device_id_type=MESH,
        )

    def height(l):
        return padded if l else g.shape[4]

    def span(l, part):
        cut = round_up(padded // 2, 8)
        return slice(cut, height(l)) if part else slice(0, cut)

    def swap_cores(l, part):
        return pltpu.make_async_remote_copy(
            src_ref=g.at[l, 1 - core, :, :, span(l, part)],
            dst_ref=r1.at[l, :, :, span(l, part)],
            send_sem=send1.at[l, part],
            recv_sem=recv1.at[l, part],
            device_id=around[0],
            device_id_type=MESH,
        )

    def swap_cols(l, part):
        return pltpu.make_async_remote_copy(
            src_ref=h.at[l, 1 - col, :, span(l, part)],
            dst_ref=r2.at[l, :, span(l, part)],
            send_sem=send2.at[l, part],
            recv_sem=recv2.at[l, part],
            device_id=around[1],
            device_id_type=MESH,
        )

    def swap_rows(l, part, hop):
        return pltpu.make_async_remote_copy(
            src_ref=k.at[l, lax.rem(row + hop, depths), span(l, part)],
            dst_ref=r3.at[l, hop - 1, span(l, part)],
            send_sem=send3.at[l, part, hop - 1],
            recv_sem=recv3.at[l, part, hop - 1],
            device_id=around[1 + hop],
            device_id_type=MESH,
        )

    def reduce_1(l):
        for d in range(peers):
            at = (l, d % 2, (d // 2) % 2, d // 4)
            g[at + (slice(0, block),)] = wacc[l, d * block : (d + 1) * block, :]
            if l == 0:
                g[at + (slice(padded, None),)] = bacc[...]
        for part in range(2):
            swap_cores(l, part).start()

    def reduce_2(l, part):
        n = span(l, part)
        swap_cores(l, part).wait_recv()
        h[l, 1 - col, :, n] = g[l, core, 1 - col, :, n] + r1[l, 1 - col, :, n]
        swap_cols(l, part).start()
        h[l, col, :, n] = g[l, core, col, :, n] + r1[l, col, :, n]

    def reduce_3(l, part):
        n = span(l, part)
        swap_cols(l, part).wait_recv()
        k[l, :, n] = h[l, col, :, n] + r2[l, :, n]
        for hop in range(1, depths):
            swap_rows(l, part, hop).start()

    def reduce_4(l, part):
        n = span(l, part)
        total = k[l, row, n]
        for hop in range(1, depths):
            swap_rows(l, part, hop).wait_recv()
            total = total + r3[l, hop - 1, n]
        last = min(n.stop, block)
        weight_grad[l, n.start : last] = scale * total[0 : last - n.start]
        if l == 0 and part == 1:
            sums = total[padded - n.start : padded - n.start + depth]
            lane = lax.broadcasted_iota(jnp.int32, sums.shape, 1)
            share = bias_grad.shape[1]
            for at in range(share):
                mine = jnp.where(lane == me * share + at, sums, 0.0)
                bias_grad[:, at : at + 1] = scale * jnp.sum(mine, axis=1, keepdims=True)

    def all_here():
        neighbours = sends_on.astype(jnp.int32) + not_last.astype(jnp.int32)
        pl.semaphore_wait(barrier, len(around) + neighbours)

    def first_pass(i, start, stop, prepares):
        def span_of(extra):
            return min(start + extra, pairs) if start else 0, min(stop + extra, pairs)

        for l in reversed(range(depth)):
            if prepares:
                prepare(l)
            if start == 0:
                load_x(l, i).wait()
            field_step(l, i, *span_of(l + 2))
            slope_step(l, i, *span_of(l + 1))
            scale_step(l, i, *span_of(l + 1))
            adjoint_step(l, i, *span_of(l))

    def send_band(i, start, stop):
        factor = gain[pl.ds(section - 1, 1), :].reshape(1, 1, 1, ch)
        for at in range(start // piece, stop // piece):
            rows = slice(at * piece, (at + 1) * piece)

            @pl.when(not_last)
            def _():
                message(i, at).wait_recv()
                corr[i, rows] = got[i, rows] - g_in[i, rows]

            msg[i, rows] = adj[i, rows] + factor * corr[i, rows]
            message(i, at).start()

    @pl.when(sends_on)
    def _():
        load_g(0).wait()
        adj[0] = g_in[0]
        bands = [(0, piece), (piece, 2 * piece), (2 * piece, pairs)]
        for start, stop in bands:
            first_pass(0, start, stop, start == 0)
            if start == 0:
                all_here()
            send_band(0, start, stop)

        @pl.loop(1, images)
        def _(i):
            load_g(i).wait()
            adj[i] = g_in[i]
            for start, stop in ((0, 2 * piece), (2 * piece, pairs)):
                first_pass(i, start, stop, False)
                send_band(i, start, stop)

    @pl.when(jnp.logical_not(sends_on))
    def _():
        @pl.loop(0, depth)
        def _(l):
            prepare(l)

        @pl.loop(0, images)
        def _(i):
            load_g(i).wait()

            @pl.loop(0, depth)
            def _(t):
                l = depth - 1 - t
                load_x(l, i).wait()
                field_step(l, i, 0, pairs)
                slope_step(l, i, 0, pairs)

        all_here()

    @pl.loop(0, images)
    def _(i):
        @pl.loop(0, depth)
        def _(l):
            turn_step(l, i)

    def begin(i, start, stop):
        @pl.when(section == 0)
        def _():
            for at in range(start // piece, stop // piece):
                message(i, at).wait_recv()

        @pl.when(not_last)
        def _():
            adj[i, start:stop] = got[i, start:stop]

    def store(i):
        return pltpu.make_async_copy(adj.at[i], starts.at[0, i], o_sem.at[i])

    for i in range(images - 1):
        begin(i, 0, pairs)

        @pl.loop(0, depth)
        def _(t):
            l = depth - 1 - t

            @pl.when(not_last)
            def _():
                scale_step(l, i, 0, pairs)
                adjoint_step(l, i, 0, pairs)

            grad_step(l, i, 0, pairs, i == 0)

        store(i).start()

    i = images - 1
    bands = [(0, 2 * piece), (2 * piece, 3 * piece), (3 * piece, pairs)]
    middle = 2 * piece

    def second_pass(l, start, stop, step):
        late = depth - 1 - l + step

        def within(at):
            return at if at in (0, pairs) else at - late

        @pl.when(not_last)
        def _():
            (adjoint_step if step else scale_step)(l, i, within(start), within(stop))

    for start, stop in bands[:-1]:
        begin(i, start, stop)
        for l in reversed(range(depth)):
            second_pass(l, start, stop, 0)
            if start:
                grad_step(l, i, 0, middle, i == 0)
            second_pass(l, start, stop, 1)

    start, stop = bands[-1]
    begin(i, start, stop)
    for l in reversed(range(depth)):
        second_pass(l, start, stop, 0)
        grad_step(l, i, middle, pairs, False)
        reduce_1(l)

        second_pass(l, start, stop, 1)
        for part in range(2):
            reduce_2(l, part)
        if l < depth - 1:
            for part in range(2):
                reduce_3(l + 1, part)
    store(i).start()
    for part in range(2):
        reduce_3(0, part)
    for l in reversed(range(depth)):
        for part in range(2):
            reduce_4(l, part)

    for i in range(images):
        store(i).wait()

        @pl.when(sends_on)
        def _():
            for at in range(pieces):
                message(i, at).wait_send()

    for l in range(depth):
        for part in range(2):
            swap_cores(l, part).wait_send()
            swap_cols(l, part).wait_send()
            for hop in range(1, depths):
                swap_rows(l, part, hop).wait_send()


def hand_over(starts, weight_grad, bias_grad, starts_out, weight_out, bias_out, a, b, c, in_sem, out_sem):
    images, pairs = starts.shape[1:3]
    parts = 4 if pairs % 4 == 0 else 1
    some = pairs // parts
    ways = [(weight_grad, b, weight_out), (bias_grad, c, bias_out)]
    for i in range(images):
        for part in range(parts):
            at = (0, i, pl.ds(part * some, some))
            ways.append((starts.at[at], a.at[at], starts_out.at[at]))
    loads = [pltpu.make_async_copy(way[0], way[1], in_sem.at[n]) for n, way in enumerate(ways)]
    stores = [pltpu.make_async_copy(way[1], way[2], out_sem.at[n]) for n, way in enumerate(ways)]
    for load in loads:
        load.start()
    for load, store in zip(loads, stores):
        load.wait()
        store.start()
    for store in stores:
        store.wait()


def per_device(sections, peers, states, weights, bias, guesses, coarse_gain):
    depth, images, high, width, ch = states.shape
    pairs = high // 2
    rows = 9 * ch // peers
    depths = peers // 4
    tall = round_up(rows, 8) + round_up(depth, 8)
    scale = step_size / (images * peers)
    f32, bf16 = jnp.float32, jnp.bfloat16
    image = (images, pairs, 2, width, ch)
    taps = (depth, images, pairs + 1, 2, width, 3 * ch)
    dma = pltpu.SemaphoreType.DMA
    conv_flops = 2 * images * high * width * 9 * ch * ch
    vmem, anywhere = pl.BlockSpec(memory_space=pltpu.VMEM), pl.BlockSpec(memory_space=pl.ANY)
    starts, weight_grad, bias_grad = pl.pallas_call(
        functools.partial(kernel, sections, peers, scale),
        out_shape=(
            jax.ShapeDtypeStruct((1,) + image, f32),
            jax.ShapeDtypeStruct((depth, rows, ch), f32),
            jax.ShapeDtypeStruct((depth, ch // peers), f32),
        ),
        in_specs=[anywhere, anywhere, vmem, anywhere, vmem],
        out_specs=(anywhere, vmem, vmem),
        scratch_shapes=[
            pltpu.VMEM((depth,) + image, bf16),
            pltpu.VMEM((depth, 9 * ch, ch), bf16),
            pltpu.VMEM(image, f32),
            pltpu.VMEM((depth, 12 * ch, 2 * ch), bf16),
            pltpu.VMEM((depth, 12 * ch, 2 * ch), bf16),
            pltpu.VMEM(taps, bf16),
            pltpu.VMEM((depth, images, 3 * ch, high * width), bf16),
            pltpu.VMEM((depth,) + image, f32),
            pltpu.VMEM(taps, bf16),
            pltpu.VMEM(image, f32),
            pltpu.VMEM(image, f32),
            pltpu.VMEM(image, f32),
            pltpu.VMEM(image, f32),
            pltpu.VMEM((depth, 9 * ch, ch), f32),
            pltpu.VMEM((round_up(depth, 8), ch), f32),
            pltpu.VMEM((depth, 2, 2, depths, tall, ch), f32),
            pltpu.VMEM((depth, 2, depths, tall, ch), f32),
            pltpu.VMEM((depth, 2, depths, tall, ch), f32),
            pltpu.VMEM((depth, depths, tall, ch), f32),
            pltpu.VMEM((depth, depths, tall, ch), f32),
            pltpu.VMEM((depth, depths, tall, ch), f32),
            dma((depth,)), dma((depth, images)), dma((images,)), dma((images,)),
            dma((images, 4)), dma((images, 4)),
            dma((depth, 2)), dma((depth, 2)), dma((depth, 2)), dma((depth, 2)),
            dma((depth, 2, depths)), dma((depth, 2, depths)),
        ],
        compiler_params=pltpu.CompilerParams(
            collective_id=0, has_side_effects=True, vmem_limit_bytes=56 * 1024 * 1024
        ),
        cost_estimate=pl.CostEstimate(
            flops=9 * conv_flops, bytes_accessed=8 * states.size, transcendentals=states.size
        ),
    )(
        states.reshape((depth,) + image),
        weights,
        bias,
        guesses.reshape((1,) + image),
        coarse_gain,
    )
    starts, weight_grad, bias_grad = pl.pallas_call(
        hand_over,
        out_shape=(
            jax.ShapeDtypeStruct(starts.shape, f32),
            jax.ShapeDtypeStruct(weight_grad.shape, f32),
            jax.ShapeDtypeStruct(bias_grad.shape, f32),
        ),
        in_specs=[anywhere] * 3,
        out_specs=(anywhere,) * 3,
        scratch_shapes=[
            pltpu.VMEM(starts.shape, f32),
            pltpu.VMEM(weight_grad.shape, f32),
            pltpu.VMEM(bias_grad.shape, f32),
            dma((images * 4 + 2,)),
            dma((images * 4 + 2,)),
        ],
        compiler_params=pltpu.CompilerParams(vmem_limit_bytes=60 * 1024 * 1024),
    )(starts, weight_grad, bias_grad)
    return starts.reshape(guesses.shape), weight_grad, bias_grad


def solution(mesh):
    return jax.shard_map(
        functools.partial(per_device, mesh.shape["layer"], mesh.shape["dp"]),
        mesh=mesh,
        in_specs=(
            P("layer", "dp", None, None, None),
            P("layer", None, None),
            P("layer", None),
            P("layer", "dp", None, None, None),
            P(),
        ),
        out_specs=(P("layer", "dp", None, None, None), P("layer", "dp", None), P("layer", "dp")),
        check_vma=False,
    )
```

```python
import functools

import jax
import jax.numpy as jnp
from jax import lax
from jax.experimental import pallas as pl
from jax.experimental.pallas import tpu as pltpu
from jax.sharding import PartitionSpec as P

MESH = pl.DeviceIdType.MESH
step_size = 0.5
parts = 3


def round_up(value, multiple):
    return -(-value // multiple) * multiple


def kernel(
    sections, peers, scale,
    states, weights, bias, guesses, gain,
    starts, weight_grad, bias_grad,
    x_in, w_in, g_in, wf, wt, x3, xt, slope, s3, adj, corr, msg, got, wacc, bacc,
    g, r1, h, r2, k, r3,
    w_sem, x_sem, g_sem, o_sem, m_send, m_recv,
    send1, recv1, send2, recv2, send3, recv3,
):
    depth, images, pairs, _, width, ch = states.shape
    depths = peers // 4
    block = weight_grad.shape[1]
    padded = round_up(block, 8)
    section = lax.axis_index("layer")
    me = lax.axis_index("dp")
    core = lax.rem(me, 2)
    col = lax.rem(lax.div(me, 2), 2)
    row = lax.div(me, 4)
    is_last = section == sections - 1
    not_last = section < sections - 1
    sends_on = section > 0

    def peer(row_at, col_at, core_at):
        return {"dp": (row_at * 2 + col_at) * 2 + core_at}

    around = [peer(row, col, 1 - core), peer(row, 1 - col, core)]
    around += [peer(lax.rem(row + hop, depths), col, core) for hop in range(1, depths)]

    def load_w(l):
        return pltpu.make_async_copy(weights.at[l], w_in.at[l], w_sem.at[l])

    def load_x(l, i):
        return pltpu.make_async_copy(states.at[l, i], x_in.at[l, i], x_sem.at[l, i])

    def load_g(i):
        return pltpu.make_async_copy(guesses.at[0, i], g_in.at[i], g_sem.at[i])

    for l in reversed(range(depth)):
        load_w(l).start()
        load_x(l, 0).start()
        if l == depth - 1:
            load_g(0).start()
    for i in range(1, images):
        for l in reversed(range(depth)):
            load_x(l, i).start()
        load_g(i).start()

    barrier = pltpu.get_barrier_semaphore()
    for target in around:
        pl.semaphore_signal(barrier, inc=1, device_id=target, device_id_type=MESH)

    @pl.when(sends_on)
    def _():
        pl.semaphore_signal(barrier, inc=1, device_id={"layer": section - 1}, device_id_type=MESH)

    @pl.when(not_last)
    def _():
        pl.semaphore_signal(barrier, inc=1, device_id={"layer": section + 1}, device_id_type=MESH)

    edge = jnp.zeros((width, 3 * ch), jnp.bfloat16)
    blank = jnp.zeros((3 * ch, ch), jnp.bfloat16)
    for l in range(depth):
        for kernels in (wf, wt):
            kernels[l, 9 * ch : 12 * ch, 0:ch] = blank
            kernels[l, 0 : 3 * ch, ch : 2 * ch] = blank
        for i in range(images):
            for field in (x3, s3):
                field[l, i, 0, 0] = edge
                field[l, i, pairs, 1] = edge

    @pl.when(is_last)
    def _():
        corr[...] = jnp.zeros_like(corr)

    bacc[...] = jnp.zeros_like(bacc)

    def prepare(l):
        load_w(l).wait()
        wf[l, 0 : 9 * ch, 0:ch] = w_in[l]
        wf[l, 3 * ch : 12 * ch, ch : 2 * ch] = w_in[l]
        for tap in range(9):
            turned = w_in[l, tap * ch : (tap + 1) * ch, :].T
            dy, dx = 2 - tap // 3, 2 - tap % 3
            for j in range(2):
                at = ((dy + j) * 3 + dx) * ch
                wt[l, at : at + ch, j * ch : (j + 1) * ch] = turned

    column = lax.broadcasted_iota(jnp.int32, (1, width, ch), 1)
    leftmost, rightmost = column == 0, column == width - 1

    def chunks(lo, hi):
        return [slice(q, min(q + 4, hi)) for q in range(lo, hi, 4)]

    def spread(field, l, i, j, q, value):
        left = jnp.where(leftmost, 0.0, pltpu.roll(value, 1, 1))
        right = jnp.where(rightmost, 0.0, pltpu.roll(value, width - 1, 1))
        at = slice(q.start + j, q.stop + j)
        field[l, i, at, 1 - j, :, 0:ch] = left.astype(jnp.bfloat16)
        field[l, i, at, 1 - j, :, ch : 2 * ch] = value.astype(jnp.bfloat16)
        field[l, i, at, 1 - j, :, 2 * ch : 3 * ch] = right.astype(jnp.bfloat16)

    def windows(field, l, i, lo, hi):
        parts = [field[l, i, pl.ds(lo + r // 2, hi - lo), r % 2] for r in range(4)]
        return jnp.concatenate(parts, axis=-1).reshape((hi - lo) * width, 12 * ch)

    def product(field, kernels, l, i, lo, hi):
        out = lax.dot_general(
            windows(field, l, i, lo, hi),
            kernels[l],
            (((1,), (0,)), ((), ())),
            preferred_element_type=jnp.float32,
        )
        for q in chunks(lo, hi):
            for j in range(2):
                at = slice((q.start - lo) * width, (q.stop - lo) * width)
                yield q, j, out[at, j * ch : (j + 1) * ch].reshape(q.stop - q.start, width, ch)

    def field_step(l, i, lo, hi):
        for q in chunks(lo, hi):
            for j in range(2):
                spread(x3, l, i, j, q, x_in[l, i, q, j].astype(jnp.float32))

    def slope_step(l, i, lo, hi):
        offset = bias[pl.ds(l, 1), :].reshape(1, 1, ch)
        for q, j, part in product(x3, wf, l, i, lo, hi):
            value = jnp.tanh(part + offset)
            slope[l, i, q, j] = 1.0 - value * value

    def scale_step(l, i, lo, hi):
        for q in chunks(lo, hi):
            for j in range(2):
                spread(s3, l, i, j, q, slope[l, i, q, j] * adj[i, q, j])

    def adjoint_step(l, i, lo, hi):
        for q, j, part in product(s3, wt, l, i, lo, hi):
            adj[i, q, j] = adj[i, q, j] + step_size * part

    def turn_step(l, i):
        flat = [x3[l, i, pl.ds(j, pairs), 1 - j].reshape(pairs * width, 3 * ch) for j in range(2)]
        for j in range(2):
            xt[l, i, :, j * pairs * width : (j + 1) * pairs * width] = flat[j].T

    def grad_step(l, i, lo, hi, first):
        rows, left = [], []
        for j in range(2):
            parts = []
            for dy in range(3):
                r = j + 2 - dy
                parts.append(s3[l, i, pl.ds(lo + r // 2, hi - lo), r % 2, :, ch : 2 * ch])
            rows.append(jnp.concatenate(parts, axis=-1).reshape((hi - lo) * width, 3 * ch))
            left.append(xt[l, i, :, (j * pairs + lo) * width : (j * pairs + hi) * width])
        right = jnp.concatenate(rows, axis=0)
        out = lax.dot_general(
            jnp.concatenate(left, axis=1),
            right,
            (((1,), (0,)), ((), ())),
            preferred_element_type=jnp.float32,
        )
        total = jnp.sum(right[:, ch : 2 * ch].astype(jnp.float32), axis=0, keepdims=True)
        bacc[pl.ds(l, 1), :] = bacc[pl.ds(l, 1), :] + total
        for dy in range(3):
            at = slice(dy * 3 * ch, (dy + 1) * 3 * ch)
            part = out[:, dy * ch : (dy + 1) * ch]
            wacc[l, at, :] = part if first else wacc[l, at, :] + part

    pieces = 4
    piece = pairs // pieces

    def message(i, at):
        return pltpu.make_async_remote_copy(
            src_ref=msg.at[i, pl.ds(at * piece, piece)],
            dst_ref=got.at[i, pl.ds(at * piece, piece)],
            send_sem=m_send.at[i, at],
            recv_sem=m_recv.at[i, at],
            device_id={"layer": section - 1},
            device_id_type=MESH,
        )

    def height(l):
        return padded if l else g.shape[4]

    def span(l, part):
        cut = round_up(-(-padded // parts), 8)
        return slice(part * cut, (part + 1) * cut if part < parts - 1 else height(l))

    def swap_cores(l, part):
        return pltpu.make_async_remote_copy(
            src_ref=g.at[l, 1 - core, :, :, span(l, part)],
            dst_ref=r1.at[l, :, :, span(l, part)],
            send_sem=send1.at[l, part],
            recv_sem=recv1.at[l, part],
            device_id=around[0],
            device_id_type=MESH,
        )

    def swap_cols(l, part):
        return pltpu.make_async_remote_copy(
            src_ref=h.at[l, 1 - col, :, span(l, part)],
            dst_ref=r2.at[l, :, span(l, part)],
            send_sem=send2.at[l, part],
            recv_sem=recv2.at[l, part],
            device_id=around[1],
            device_id_type=MESH,
        )

    def swap_rows(l, part, hop):
        return pltpu.make_async_remote_copy(
            src_ref=k.at[l, lax.rem(row + hop, depths), span(l, part)],
            dst_ref=r3.at[l, hop - 1, span(l, part)],
            send_sem=send3.at[l, part, hop - 1],
            recv_sem=recv3.at[l, part, hop - 1],
            device_id=around[1 + hop],
            device_id_type=MESH,
        )

    def reduce_1(l):
        for d in range(peers):
            at = (l, d % 2, (d // 2) % 2, d // 4)
            g[at + (slice(0, block),)] = wacc[l, d * block : (d + 1) * block, :]
            if l == 0:
                g[at + (slice(padded, None),)] = bacc[...]
        for part in range(parts):
            swap_cores(l, part).start()

    def reduce_2(l, part):
        n = span(l, part)
        swap_cores(l, part).wait_recv()
        h[l, 1 - col, :, n] = g[l, core, 1 - col, :, n] + r1[l, 1 - col, :, n]
        swap_cols(l, part).start()
        h[l, col, :, n] = g[l, core, col, :, n] + r1[l, col, :, n]

    def reduce_3(l, part):
        n = span(l, part)
        swap_cols(l, part).wait_recv()
        k[l, :, n] = h[l, col, :, n] + r2[l, :, n]
        for hop in range(1, depths):
            swap_rows(l, part, hop).start()

    def reduce_4(l, part):
        n = span(l, part)
        total = k[l, row, n]
        for hop in range(1, depths):
            swap_rows(l, part, hop).wait_recv()
            total = total + r3[l, hop - 1, n]
        last = min(n.stop, block)
        weight_grad[l, n.start : last] = scale * total[0 : last - n.start]
        if l == 0 and part == parts - 1:
            sums = total[padded - n.start : padded - n.start + depth]
            lane = lax.broadcasted_iota(jnp.int32, sums.shape, 1)
            share = bias_grad.shape[1]
            for at in range(share):
                mine = jnp.where(lane == me * share + at, sums, 0.0)
                bias_grad[:, at : at + 1] = scale * jnp.sum(mine, axis=1, keepdims=True)

    def all_here():
        neighbours = sends_on.astype(jnp.int32) + not_last.astype(jnp.int32)
        pl.semaphore_wait(barrier, len(around) + neighbours)

    def first_pass(i, start, stop, prepares):
        def span_of(extra):
            return min(start + extra, pairs) if start else 0, min(stop + extra, pairs)

        for l in reversed(range(depth)):
            if prepares:
                prepare(l)
            if start == 0:
                load_x(l, i).wait()
            field_step(l, i, *span_of(l + 2))
            slope_step(l, i, *span_of(l + 1))
            scale_step(l, i, *span_of(l + 1))
            adjoint_step(l, i, *span_of(l))

    def send_band(i, start, stop):
        factor = gain[pl.ds(section - 1, 1), :].reshape(1, 1, 1, ch)
        for at in range(start // piece, stop // piece):
            rows = slice(at * piece, (at + 1) * piece)

            @pl.when(not_last)
            def _():
                message(i, at).wait_recv()
                corr[i, rows] = got[i, rows] - g_in[i, rows]

            msg[i, rows] = adj[i, rows] + factor * corr[i, rows]
            message(i, at).start()

    @pl.when(sends_on)
    def _():
        load_g(0).wait()
        adj[0] = g_in[0]
        bands = [(0, piece), (piece, 2 * piece), (2 * piece, pairs)]
        for start, stop in bands:
            first_pass(0, start, stop, start == 0)
            if start == 0:
                all_here()
            send_band(0, start, stop)

        @pl.loop(1, images)
        def _(i):
            load_g(i).wait()
            adj[i] = g_in[i]
            for start, stop in ((0, 2 * piece), (2 * piece, pairs)):
                first_pass(i, start, stop, False)
                send_band(i, start, stop)

    @pl.when(jnp.logical_not(sends_on))
    def _():
        @pl.loop(0, depth)
        def _(l):
            prepare(l)

        @pl.loop(0, images)
        def _(i):
            load_g(i).wait()

            @pl.loop(0, depth)
            def _(t):
                l = depth - 1 - t
                load_x(l, i).wait()
                field_step(l, i, 0, pairs)
                slope_step(l, i, 0, pairs)

        all_here()

    @pl.loop(0, images)
    def _(i):
        @pl.loop(0, depth)
        def _(l):
            turn_step(l, i)

    def begin(i, start, stop):
        @pl.when(section == 0)
        def _():
            for at in range(start // piece, stop // piece):
                message(i, at).wait_recv()

        @pl.when(not_last)
        def _():
            adj[i, start:stop] = got[i, start:stop]

    def store(i):
        return pltpu.make_async_copy(adj.at[i], starts.at[0, i], o_sem.at[i])

    for i in range(images - 1):
        begin(i, 0, pairs)

        @pl.loop(0, depth)
        def _(t):
            l = depth - 1 - t

            @pl.when(not_last)
            def _():
                scale_step(l, i, 0, pairs)
                adjoint_step(l, i, 0, pairs)

            grad_step(l, i, 0, pairs, i == 0)

        store(i).start()

    i = images - 1
    bands = [(0, 2 * piece), (2 * piece, 3 * piece), (3 * piece, pairs)]
    middle = 2 * piece

    def second_pass(l, start, stop, step):
        late = depth - 1 - l + step

        def within(at):
            return at if at in (0, pairs) else at - late

        @pl.when(not_last)
        def _():
            (adjoint_step if step else scale_step)(l, i, within(start), within(stop))

    for start, stop in bands[:-1]:
        begin(i, start, stop)
        for l in reversed(range(depth)):
            second_pass(l, start, stop, 0)
            if start:
                grad_step(l, i, 0, middle, i == 0)
            second_pass(l, start, stop, 1)

    start, stop = bands[-1]
    begin(i, start, stop)
    for l in reversed(range(depth)):
        second_pass(l, start, stop, 0)
        grad_step(l, i, middle, pairs, False)
        reduce_1(l)

        second_pass(l, start, stop, 1)
        for part in range(parts):
            reduce_2(l, part)
        if l < depth - 1:
            for part in range(parts):
                reduce_3(l + 1, part)
    store(i).start()
    for part in range(parts):
        reduce_3(0, part)
    for l in reversed(range(depth)):
        for part in range(parts):
            reduce_4(l, part)

    for i in range(images):
        store(i).wait()

        @pl.when(sends_on)
        def _():
            for at in range(pieces):
                message(i, at).wait_send()

    for l in range(depth):
        for part in range(parts):
            swap_cores(l, part).wait_send()
            swap_cols(l, part).wait_send()
            for hop in range(1, depths):
                swap_rows(l, part, hop).wait_send()


def hand_over(starts, weight_grad, bias_grad, starts_out, weight_out, bias_out, a, b, c, in_sem, out_sem):
    images, pairs = starts.shape[1:3]
    slabs = 4 if pairs % 4 == 0 else 1
    some = pairs // slabs
    ways = [(weight_grad, b, weight_out), (bias_grad, c, bias_out)]
    for i in range(images):
        for slab in range(slabs):
            at = (0, i, pl.ds(slab * some, some))
            ways.append((starts.at[at], a.at[at], starts_out.at[at]))
    loads = [pltpu.make_async_copy(way[0], way[1], in_sem.at[n]) for n, way in enumerate(ways)]
    stores = [pltpu.make_async_copy(way[1], way[2], out_sem.at[n]) for n, way in enumerate(ways)]
    for load in loads:
        load.start()
    for load, store in zip(loads, stores):
        load.wait()
        store.start()
    for store in stores:
        store.wait()


def per_device(sections, peers, states, weights, bias, guesses, coarse_gain):
    depth, images, high, width, ch = states.shape
    pairs = high // 2
    rows = 9 * ch // peers
    depths = peers // 4
    tall = round_up(rows, 8) + round_up(depth, 8)
    scale = step_size / (images * peers)
    f32, bf16 = jnp.float32, jnp.bfloat16
    image = (images, pairs, 2, width, ch)
    taps = (depth, images, pairs + 1, 2, width, 3 * ch)
    dma = pltpu.SemaphoreType.DMA
    conv_flops = 2 * images * high * width * 9 * ch * ch
    vmem, anywhere = pl.BlockSpec(memory_space=pltpu.VMEM), pl.BlockSpec(memory_space=pl.ANY)
    starts, weight_grad, bias_grad = pl.pallas_call(
        functools.partial(kernel, sections, peers, scale),
        out_shape=(
            jax.ShapeDtypeStruct((1,) + image, f32),
            jax.ShapeDtypeStruct((depth, rows, ch), f32),
            jax.ShapeDtypeStruct((depth, ch // peers), f32),
        ),
        in_specs=[anywhere, anywhere, vmem, anywhere, vmem],
        out_specs=(anywhere, vmem, vmem),
        scratch_shapes=[
            pltpu.VMEM((depth,) + image, bf16),
            pltpu.VMEM((depth, 9 * ch, ch), bf16),
            pltpu.VMEM(image, f32),
            pltpu.VMEM((depth, 12 * ch, 2 * ch), bf16),
            pltpu.VMEM((depth, 12 * ch, 2 * ch), bf16),
            pltpu.VMEM(taps, bf16),
            pltpu.VMEM((depth, images, 3 * ch, high * width), bf16),
            pltpu.VMEM((depth,) + image, f32),
            pltpu.VMEM(taps, bf16),
            pltpu.VMEM(image, f32),
            pltpu.VMEM(image, f32),
            pltpu.VMEM(image, f32),
            pltpu.VMEM(image, f32),
            pltpu.VMEM((depth, 9 * ch, ch), f32),
            pltpu.VMEM((round_up(depth, 8), ch), f32),
            pltpu.VMEM((depth, 2, 2, depths, tall, ch), f32),
            pltpu.VMEM((depth, 2, depths, tall, ch), f32),
            pltpu.VMEM((depth, 2, depths, tall, ch), f32),
            pltpu.VMEM((depth, depths, tall, ch), f32),
            pltpu.VMEM((depth, depths, tall, ch), f32),
            pltpu.VMEM((depth, depths, tall, ch), f32),
            dma((depth,)), dma((depth, images)), dma((images,)), dma((images,)),
            dma((images, 4)), dma((images, 4)),
            dma((depth, parts)), dma((depth, parts)), dma((depth, parts)), dma((depth, parts)),
            dma((depth, parts, depths)), dma((depth, parts, depths)),
        ],
        compiler_params=pltpu.CompilerParams(
            collective_id=0, has_side_effects=True, vmem_limit_bytes=56 * 1024 * 1024
        ),
        cost_estimate=pl.CostEstimate(
            flops=9 * conv_flops, bytes_accessed=8 * states.size, transcendentals=states.size
        ),
    )(
        states.reshape((depth,) + image),
        weights,
        bias,
        guesses.reshape((1,) + image),
        coarse_gain,
    )
    starts, weight_grad, bias_grad = pl.pallas_call(
        hand_over,
        out_shape=(
            jax.ShapeDtypeStruct(starts.shape, f32),
            jax.ShapeDtypeStruct(weight_grad.shape, f32),
            jax.ShapeDtypeStruct(bias_grad.shape, f32),
        ),
        in_specs=[anywhere] * 3,
        out_specs=(anywhere,) * 3,
        scratch_shapes=[
            pltpu.VMEM(starts.shape, f32),
            pltpu.VMEM(weight_grad.shape, f32),
            pltpu.VMEM(bias_grad.shape, f32),
            dma((images * 4 + 2,)),
            dma((images * 4 + 2,)),
        ],
        compiler_params=pltpu.CompilerParams(vmem_limit_bytes=60 * 1024 * 1024),
    )(starts, weight_grad, bias_grad)
    return starts.reshape(guesses.shape), weight_grad, bias_grad


def solution(mesh):
    return jax.shard_map(
        functools.partial(per_device, mesh.shape["layer"], mesh.shape["dp"]),
        mesh=mesh,
        in_specs=(
            P("layer", "dp", None, None, None),
            P("layer", None, None),
            P("layer", None),
            P("layer", "dp", None, None, None),
            P(),
        ),
        out_specs=(P("layer", "dp", None, None, None), P("layer", "dp", None), P("layer", "dp")),
        check_vma=False,
    )
```
